32 devices in a mesh: dp: 4 (over x, core), ctx: 8 (over z, y).
Axes of the slice: x: 2, y: 2, z: 4, core: 2. Of those that a mesh axis runs over, the one named last changes fastest.
Arguments:
- tokens: bfloat16 [4, 2, 8, 64, 2048], P('dp', None, 'ctx'), may hold values from -6 to 6
- norm_gain: bfloat16 [2048], P(('dp', 'ctx')), may hold values from 0.5 to 1.5
- norm_shift: bfloat16 [2048], P(('dp', 'ctx')), may hold values from -0.5 to 0.5
- input_weight: bfloat16 [2048, 14336], P(('dp', 'ctx')), may hold values from -0.1875 to 0.1875
- input_bias: bfloat16 [14336], P(('dp', 'ctx')), may hold values from -0.5 to 0.5
- output_weight: bfloat16 [10240, 2048], P(('dp', 'ctx')), may hold values from -0.0625 to 0.0625
- output_bias: bfloat16 [2048], P(('dp', 'ctx')), may hold values from -0.5 to 0.5
- cotangent: bfloat16 [4, 2, 8, 64, 2048], P('dp', None, 'ctx'), may hold values from -6 to 6
Outputs:
- block_out: bfloat16 [4, 2, 8, 64, 2048], P('dp', None, 'ctx')
- tokens_grad: float32 [4, 2, 8, 64, 2048], P('dp', None, 'ctx')
- gain_grad: float32 [2048], P(('dp', 'ctx'))
- shift_grad: float32 [2048], P(('dp', 'ctx'))
- weightin_grad: float32 [2048, 14336], P(('dp', 'ctx'))
- biasin_grad: float32 [14336], P(('dp', 'ctx'))
- weightout_grad: float32 [10240, 2048], P(('dp', 'ctx'))
- biasout_grad: float32 [2048], P(('dp', 'ctx'))
The draws below stay inside these ranges and needn't reach their ends.
All inputs are finite; a program needn't handle non-finite values.
Results may differ from the reference program's by a relative error of at most 0.0081.
Values may be sent and summed in bfloat16 or wider, within the bound.
No kernel may reach another device: no remote copies, remote signals or barrier semaphores. Data moves between devices by JAX's collectives and lax.ppermute only.
A program may use at most 512 MiB of HBM per device.

```python
import math
import jax
import jax.numpy as jnp
from jax import lax

D = 2048
FF = 8192
HEADS = 32
HEAD = 64
ROT = 32
BLK = 64
SEQS = 4
N_CTX = 8


def level_of(key, shape, pieces, least, high):
    factor_of, own = 1.0, jax.random.fold_in(key, 6)
    for position, shards_of in pieces:
        heights = jnp.exp(jax.random.uniform(jax.random.fold_in(own, position), (shards_of,), jnp.float32, least / len(pieces), high / len(pieces)))
        factor_of = factor_of * jnp.repeat(heights, shape[position] // shards_of).reshape([-1 if axis == position else 1 for axis in range(len(shape))])
    return factor_of


def scatter_about(stream_key, dims, scale, reach, shards=(), held_as=jnp.bfloat16):
    values = scale * jax.random.normal(stream_key, dims, jnp.float32)
    if shards:
        values = values * level_of(stream_key, dims, shards, -0.22, 0.18)
    return jnp.clip(values, -reach, reach).astype(held_as)


def setup_inputs(seed: int = 0) -> dict:
    arg_keys = jax.random.split(jax.random.key(seed), 9)
    return {
        "tokens": scatter_about(arg_keys[0], (SEQS, 2, N_CTX, BLK, D), 1.0, 6.0, ((0, 4), (2, 8))),
        "norm_gain": jnp.clip(1.0 + 0.1 * jax.random.normal(arg_keys[1], (D,), jnp.float32), 0.5, 1.5).astype(jnp.bfloat16),
        "norm_shift": jnp.clip(jax.random.uniform(arg_keys[2], (D,), jnp.float32, -0.5, 0.5) * level_of(arg_keys[2], (D,), ((0, 32),), -0.4, 0.0), -0.5, 0.5).astype(jnp.bfloat16),
        "input_weight": scatter_about(arg_keys[3], (D, 3 * D + FF), (D // 2) ** -0.5, 0.1875, ((0, 32),)),
        "input_bias": jnp.clip(jax.random.uniform(arg_keys[4], (3 * D + FF,), jnp.float32, -0.5, 0.5) * level_of(arg_keys[4], (3 * D + FF,), ((0, 32),), -0.4, 0.0), -0.5, 0.5).astype(jnp.bfloat16),
        "output_weight": scatter_about(arg_keys[5], (D + FF, D), FF ** -0.5, 0.0625, ((0, 32),)),
        "output_bias": jnp.clip(jax.random.uniform(arg_keys[6], (D,), jnp.float32, -0.5, 0.5) * level_of(arg_keys[6], (D,), ((0, 32),), -0.4, 0.0), -0.5, 0.5).astype(jnp.bfloat16),
        "cotangent": scatter_about(arg_keys[7], (SEQS, 2, N_CTX, BLK, D), 1.0, 6.0, ((0, 4), (2, 8))),
    }


@jax.custom_vjp
def low(v):
    return lax.optimization_barrier(v.astype(jnp.bfloat16)).astype(jnp.float32)

@jax.custom_vjp
def low_back(v):
    return v

def low_keep(v):
    return (low(v), None)

def low_pass(kept, grad):
    return (grad,)

def back_keep(v):
    return (v, None)

def back_low(kept, grad):
    return (low(grad),)
low.defvjp(low_keep, low_pass)
low_back.defvjp(back_keep, back_low)
epsilon = 1e-05
theta_log = math.log(10000.0)
masked_fill = -1e+30
highest = lax.Precision.HIGHEST

def layer_norm(values, norm_gain, norm_shift):
    middle = lax.optimization_barrier(jnp.mean(values, axis=-1, keepdims=True))
    centred = values - middle
    spread = lax.optimization_barrier(jnp.mean(centred * centred, axis=-1, keepdims=True))
    return centred * lax.rsqrt(spread + epsilon) * norm_gain + norm_shift

def turn_heads(values, angles):
    half_rot = ROT // 2
    former = values[..., :half_rot]
    latter = values[..., half_rot:ROT]
    cosine = jnp.cos(angles)[:, None, :]
    sine_table = jnp.sin(angles)[:, None, :]
    return jnp.concatenate([former * cosine - latter * sine_table, latter * cosine + former * sine_table, values[..., ROT:]], axis=-1)

def angle_table(positions):
    frequency = jnp.exp(-theta_log * 2.0 * jnp.arange(ROT // 2).astype(jnp.float32) / ROT)
    return positions.astype(jnp.float32)[:, None] * frequency[None, :]

def forward(inputs, norm_gain, norm_shift, input_weight, input_bias, output_weight, output_bias):
    length = inputs.shape[0]
    normed = low(layer_norm(inputs, norm_gain, norm_shift))
    hidden = low_back(jnp.dot(normed, input_weight, precision=highest) + input_bias)
    angles = angle_table(jnp.arange(length, dtype=jnp.int32))
    queries = low(turn_heads(hidden[:, :D].reshape(length, HEADS, HEAD), angles))
    key_rows = low(turn_heads(hidden[:, D:2 * D].reshape(length, HEADS, HEAD), angles))
    values = low(hidden[:, 2 * D:3 * D].reshape(length, HEADS, HEAD))
    rows_block = math.gcd(length, 512)
    key_pos = jnp.arange(length, dtype=jnp.int32)

    def attend(start):
        block_q = lax.dynamic_slice_in_dim(queries, start, rows_block, 0)
        scores = low_back(jnp.einsum('qhe,khe->hqk', block_q, key_rows, precision=highest) * 0.125)
        row_pos = start + jnp.arange(rows_block, dtype=jnp.int32)
        allowed = key_pos[None, :] <= row_pos[:, None]
        scores = jnp.where(allowed[None], scores, masked_fill)
        row_top = lax.optimization_barrier(jnp.max(scores, axis=-1, keepdims=True))
        weights = jnp.exp(scores - row_top)
        shares = low(weights / lax.optimization_barrier(jnp.sum(weights, axis=-1, keepdims=True)))
        return jnp.einsum('hqk,khe->qhe', shares, values, precision=highest)
    starts = (jnp.arange(length // rows_block, dtype=jnp.int32) * rows_block).astype(jnp.int32)
    mixture = lax.map(jax.checkpoint(attend), starts).reshape(length, D)
    attended = low_back(mixture)
    activated = jax.nn.gelu(hidden[:, 3 * D:], approximate=True)
    branch = low(jnp.concatenate([attended, activated], axis=-1))
    return inputs + jnp.dot(branch, output_weight, precision=highest) + output_bias

def reference(tokens, norm_gain, norm_shift, input_weight, input_bias, output_weight, output_bias, cotangent):
    length = 2 * BLK * N_CTX
    params = tuple((entry.astype(jnp.float32) for entry in (norm_gain, norm_shift, input_weight, input_bias, output_weight, output_bias)))

    def natural(stored):
        return jnp.concatenate([stored[0], stored[1][::-1]], axis=0).reshape(length, stored.shape[-1])

    def storage(flat_rows):
        blocks = flat_rows.reshape(2 * N_CTX, BLK, flat_rows.shape[-1])
        return jnp.stack([blocks[:N_CTX], blocks[N_CTX:][::-1]])

    def one_sequence(totals, sequence_pair):
        stored, cot_rows = sequence_pair
        result, pullback = jax.vjp(forward, natural(stored), *params)
        gradients = pullback(natural(cot_rows))
        totals = tuple((running + gradient for running, gradient in zip(totals, gradients[1:])))
        return (totals, (storage(result), storage(gradients[0])))
    zeros = tuple((jnp.zeros_like(entry) for entry in params))
    sums, (outputs, input_grads) = lax.scan(one_sequence, zeros, (tokens.astype(jnp.float32), cotangent.astype(jnp.float32)))
    return (outputs.astype(jnp.bfloat16), input_grads, sums[0], sums[1], sums[2], sums[3], sums[4], sums[5])
```

```python
import functools
import math

import jax
import jax.numpy as jnp
from jax import lax
from jax.experimental import pallas as pl
from jax.experimental.pallas import tpu as pltpu
from jax.sharding import PartitionSpec as P

D = 2048
HEADS = 32
HEAD = 64
ROT = 32
BLK = 64
FF = 8192
TILE = 256

epsilon = 1e-05
theta_log = math.log(10000.0)
masked_fill = -1e30
bf16 = jnp.bfloat16
f32 = jnp.float32


def dot(a, b, dims):
    return lax.dot_general(a, b, (dims, ((), ())), preferred_element_type=f32)


def turn_lanes(values, cos, sin, lanes, sign):
    half = ROT // 2
    width = values.shape[-1]
    place = lanes % HEAD
    ahead = pltpu.roll(values, width - half, 1)
    behind = pltpu.roll(values, half, 1)
    turned = values * cos + sign * sin * jnp.where(place < half, -ahead, behind)
    return jnp.where(place < ROT, turned, values)


def attention_kernel(length, width, hq, hk, hv, gm, cos, sin, att, gq, gk, gv, qs, ks, vs, kt, vt, dk, dv):
    lanes = lax.broadcasted_iota(jnp.int32, (1, width), 1)
    tile = min(TILE, length)
    cos_all, sin_all = cos[...], sin[...]
    turn = functools.partial(turn_lanes, cos=cos_all, sin=sin_all, lanes=lanes)
    qs[...] = turn(hq[...], sign=1.0).astype(bf16)
    turned_keys = turn(hk[...], sign=1.0)
    ks[...] = turned_keys.astype(bf16)
    kt[...] = turned_keys.T.astype(bf16)
    values = hv[...]
    vs[...] = values.astype(bf16)
    vt[...] = values.T.astype(bf16)
    dk[...] = jnp.zeros_like(dk)
    dv[...] = jnp.zeros_like(dv)
    causal = lax.broadcasted_iota(jnp.int32, (tile, tile), 0) <= lax.broadcasted_iota(
        jnp.int32, (tile, tile), 1
    )

    def rows_step(start, reach):
        rows = pl.ds(start, tile)
        q_rows = qs[rows, :]
        g_rows = gm[rows, :]
        keys = ks[0:reach, :]
        vals = vs[0:reach, :]
        mixes, gqs = [], []
        if reach == tile:
            allowed = causal
        else:
            allowed = lax.broadcasted_iota(jnp.int32, (reach, tile), 0) <= start + (
                lax.broadcasted_iota(jnp.int32, (reach, tile), 1)
            )
        for head in range(width // HEAD):
            mine = (lanes // HEAD) == head
            q_head = jnp.where(mine, q_rows, jnp.zeros_like(q_rows))
            g_head = jnp.where(mine, g_rows, jnp.zeros_like(g_rows))
            span = slice(head * HEAD, (head + 1) * HEAD)
            scores = dot(keys, q_head, ((1,), (1,))) * 0.125
            scores = jnp.where(allowed, scores, masked_fill)
            top = jnp.max(scores, axis=0, keepdims=True)
            weights = jnp.exp(scores - top)
            total = jnp.sum(weights, axis=0, keepdims=True)
            shares = weights * (1.0 / total)
            low = shares.astype(bf16)
            grad_shares = dot(vals, g_head, ((1,), (1,)))
            moved = shares * grad_shares
            inner = jnp.sum(moved, axis=0, keepdims=True)
            grad_scores = (moved - shares * inner).astype(bf16)
            mixes.append(dot(vt[span, 0:reach], low, ((1,), (0,))))
            gqs.append(dot(kt[span, 0:reach], grad_scores, ((1,), (0,))))
            dv[0:reach, :] += dot(low, g_head, ((1,), (0,)))
            dk[0:reach, :] += dot(grad_scores, q_head, ((1,), (0,)))
        att[rows, :] = jnp.concatenate(mixes, axis=0).T.astype(bf16)
        grad_q = jnp.concatenate(gqs, axis=0).T * 0.125
        gq[rows, :] = turn_lanes(grad_q, cos[rows, :], sin[rows, :], lanes, -1.0).astype(bf16)

    count = length // tile
    if count <= 4:
        for step in range(count):
            rows_step(step * tile, (step + 1) * tile)
    else:
        per = count // 4
        for part in range(4):

            @pl.loop(part * per, (part + 1) * per)
            def _(step, part=part):
                rows_step(pl.multiple_of(step * tile, tile), (part + 1) * per * tile)

    gk[...] = turn(dk[...] * 0.125, sign=-1.0).astype(bf16)
    gv[...] = dv[...].astype(bf16)


def attention(hidden, grad_mix):
    length, columns = grad_mix.shape
    width = min(128, columns)
    groups = columns // width
    frequency = jnp.exp(-theta_log * 2.0 * jnp.arange(ROT // 2).astype(f32) / ROT)
    angles = jnp.arange(length, dtype=jnp.int32).astype(f32)[:, None] * frequency[None, :]
    spare = jnp.zeros((length, HEAD - ROT), f32)
    repeat = width // HEAD
    cos = jnp.tile(jnp.concatenate([jnp.cos(angles)] * 2 + [spare], axis=1), (1, repeat))
    sin = jnp.tile(jnp.concatenate([jnp.sin(angles)] * 2 + [spare], axis=1), (1, repeat))
    third = lambda which: pl.BlockSpec((length, width), lambda g: (0, which * groups + g))
    group = pl.BlockSpec((length, width), lambda g: (0, g))
    table = pl.BlockSpec((length, width), lambda g: (0, 0))
    out = jax.ShapeDtypeStruct((length, columns), bf16)
    if width < 128:
        parts = [hidden[:, k * columns : (k + 1) * columns] for k in range(3)]
        specs = [group] * 3
    else:
        parts = [hidden] * 3
        specs = [third(0), third(1), third(2)]
    pairs = length * length * columns // 2
    return pl.pallas_call(
        functools.partial(attention_kernel, length, width),
        grid=(groups,),
        in_specs=specs + [group, table, table],
        out_specs=[group] * 4,
        out_shape=[out] * 4,
        scratch_shapes=[
            pltpu.VMEM((length, width), bf16),
            pltpu.VMEM((length, width), bf16),
            pltpu.VMEM((length, width), bf16),
            pltpu.VMEM((width, length), bf16),
            pltpu.VMEM((width, length), bf16),
            pltpu.VMEM((length, width), f32),
            pltpu.VMEM((length, width), f32),
        ],
        compiler_params=pltpu.CompilerParams(vmem_limit_bytes=56 * 2**20),
        cost_estimate=pl.CostEstimate(
            flops=14 * pairs * 2, bytes_accessed=length * columns * 30, transcendentals=pairs // HEAD
        ),
        name="attention",
    )(*parts, grad_mix, cos, sin)


def shift_pairs(size, by):
    return [(k, (k + by) % size) for k in range(size)]


def flip_pairs(size, bit):
    return [(k, k ^ bit) for k in range(size)]


def gather_small(vector):
    held = vector[None]
    for axis in ("ctx", "dp"):
        size = lax.axis_size(axis)
        place = lax.axis_index(axis)
        bit = 1
        while bit < size:
            other = lax.ppermute(held, axis, flip_pairs(size, bit))
            upper = (place & bit) != 0
            held = jnp.where(
                upper, jnp.concatenate([other, held]), jnp.concatenate([held, other])
            )
            bit *= 2
    return held


def scatter_small(terms):
    held = terms
    for axis in ("dp", "ctx"):
        size = lax.axis_size(axis)
        place = lax.axis_index(axis)
        bit = size // 2
        while bit >= 1:
            half = held.shape[0] // 2
            low, high = held[:half], held[half:]
            upper = (place & bit) != 0
            other = lax.ppermute(jnp.where(upper, low, high), axis, flip_pairs(size, bit))
            held = jnp.where(upper, high, low) + other
            bit //= 2
    return held[0]


def put_rows(buffer, block, index, count):
    buffer = lax.dynamic_update_slice(buffer, block[:BLK], (index * BLK, 0))
    return lax.dynamic_update_slice(buffer, block[BLK:], ((2 * count - 1 - index) * BLK, 0))


def take_rows(array, index, count):
    former = lax.dynamic_slice_in_dim(array, index * BLK, BLK, 0)
    latter = lax.dynamic_slice_in_dim(array, (2 * count - 1 - index) * BLK, BLK, 0)
    return jnp.concatenate([former, latter], axis=0)


def gather_rows(block):
    count = lax.axis_size("ctx")
    place = lax.axis_index("ctx")
    far = count // 2
    total = jnp.zeros((count * 2 * BLK, block.shape[1]), block.dtype)
    held = block
    for step in range(far):
        if step:
            held = lax.ppermute(held, "ctx", shift_pairs(count, 2))
        owner = (place + count - 2 * step) % count
        other = lax.ppermute(held, "ctx", flip_pairs(count, 1))
        total = put_rows(total, held, owner, count)
        total = put_rows(total, other, owner ^ 1, count)
    return total


def scatter_rows(terms):
    count = lax.axis_size("ctx")
    place = lax.axis_index("ctx")
    far = count // 2
    total = None
    for step in [*range(1, far), 0]:
        owner = (place + 2 * step) % count
        other = lax.ppermute(
            take_rows(terms, owner ^ 1, count).astype(bf16), "ctx", flip_pairs(count, 1)
        )
        joint = take_rows(terms, owner, count) + other.astype(f32)
        if step:
            joint = lax.ppermute(joint.astype(bf16), "ctx", shift_pairs(count, 2 * step)).astype(f32)
        total = joint if total is None else total + joint
    return total


def column_pieces(index, count):
    own = D // count
    rows = (D + FF) // (4 * count)
    pieces = [(which * D + index * own, own) for which in range(3)]
    pieces.append((3 * D + index * (rows - own), rows - own))
    for part in range(1, 4):
        pieces.append((3 * D + part * rows * count - D + index * rows, rows))
    return pieces


def take_columns(array, index, count, pieces):
    parts = [
        lax.dynamic_slice_in_dim(array, start, width, 1)
        for start, width in column_pieces(index, count)[pieces]
    ]
    return jnp.concatenate(parts, axis=1)


def spread_columns(array, pieces):
    count = lax.axis_size("ctx")
    place = lax.axis_index("ctx")
    rows = array.shape[0]
    own = take_columns(array, place, count, pieces)
    total = jnp.zeros((count, rows, own.shape[1]), array.dtype)
    total = lax.dynamic_update_slice(total, own[None], (place, 0, 0))
    for step in range(1, count):
        sent = take_columns(array, (place + step) % count, count, pieces)
        got = lax.ppermute(sent, "ctx", shift_pairs(count, step))
        total = lax.dynamic_update_slice(total, got[None], ((place + count - step) % count, 0, 0))
    return total.reshape(count * rows, -1)


def collect_columns(output, array, pieces):
    count = lax.axis_size("ctx")
    place = lax.axis_index("ctx")
    rows = output.shape[0]

    def put(output, block, index):
        at = 0
        for start, width in column_pieces(index, count)[pieces]:
            output = lax.dynamic_update_slice(output, block[:, at : at + width], (0, start))
            at += width
        return output

    output = put(output, lax.dynamic_slice_in_dim(array, place * rows, rows, 0), place)
    for step in range(1, count):
        sent = lax.dynamic_slice_in_dim(array, ((place + step) % count) * rows, rows, 0)
        got = lax.ppermute(sent.astype(bf16), "ctx", shift_pairs(count, step))
        output = put(output, got.astype(f32), (place + count - step) % count)
    return output


def gather_dp(block):
    place = lax.axis_index("dp")
    rows = block.shape[0]
    total = jnp.zeros((4, *block.shape), block.dtype)
    across = lax.ppermute(block, "dp", flip_pairs(4, 2))
    total = lax.dynamic_update_slice(total, block[None], (place, 0, 0))
    total = lax.dynamic_update_slice(total, across[None], (place ^ 2, 0, 0))
    beside = lax.ppermute(block, "dp", flip_pairs(4, 1))
    total = lax.dynamic_update_slice(total, beside[None], (place ^ 1, 0, 0))
    beyond = lax.ppermute(across, "dp", flip_pairs(4, 1))
    total = lax.dynamic_update_slice(total, beyond[None], (place ^ 3, 0, 0))
    return total.reshape(4 * rows, -1)


def scatter_dp(terms):
    place = lax.axis_index("dp")
    rows = terms.shape[0] // 4
    part = lambda index: lax.dynamic_slice_in_dim(terms, index * rows, rows, 0)
    sent_far = part(place ^ 3).astype(bf16)
    got_far = lax.ppermute(sent_far, "dp", flip_pairs(4, 1))
    far = part(place ^ 2) + got_far.astype(f32)
    got_near = lax.ppermute(part(place ^ 1).astype(bf16), "dp", flip_pairs(4, 1))
    near = part(place) + got_near.astype(f32)
    got = lax.ppermute(far.astype(bf16), "dp", flip_pairs(4, 2))
    return near + got.astype(f32)


def unit_rounds(count):
    edges = []
    for m in range(5 * count):
        owner, slot = (m // 4, m % 4) if m < 4 * count else (m - 4 * count, 4)
        edges.append((m // 5, m % 5, owner, slot))
    rounds = []
    left = list(edges)
    for _ in range(5):
        by_source = [[e for e in left if e[0] == s] for s in range(count)]
        taken = {}

        def place_edge(source, seen):
            for edge in by_source[source]:
                if edge[2] in seen:
                    continue
                seen.add(edge[2])
                if edge[2] not in taken or place_edge(taken[edge[2]][0], seen):
                    taken[edge[2]] = edge
                    return True
            return False

        for source in range(count):
            assert place_edge(source, set())
        chosen = {edge[0]: edge for edge in taken.values()}
        rounds.append([chosen[s] for s in range(count)])
        for edge in taken.values():
            left.remove(edge)
    return rounds


def swap_units(block, back):
    count = lax.axis_size("ctx")
    place = lax.axis_index("ctx")
    first = lax.axis_index("dp") == 0
    rows = block.shape[0] // 5
    total = jnp.zeros_like(block)
    for chosen in unit_rounds(count):
        out_unit, in_unit, pairs = [0] * count, [0] * count, []
        for source, unit, owner, slot in chosen:
            if back:
                source, unit, owner, slot = owner, slot, source, unit
            pairs.append((source, owner))
            out_unit[source] = unit
            in_unit[owner] = slot
        sent = lax.dynamic_slice_in_dim(block, jnp.array(out_unit)[place] * rows, rows, 0)
        got = lax.ppermute(sent, ("dp", "ctx"), pairs)
        total = lax.dynamic_update_slice(total, got, (jnp.array(in_unit)[place] * rows, 0))
    return jnp.where(first, total, block)


def local(
    tokens, norm_gain, norm_shift, input_weight, input_bias, output_weight, output_bias, cotangent
):
    count = lax.axis_size("ctx")
    place = lax.axis_index("ctx")
    devices = 4 * count
    own = D // count
    qkv = slice(0, 3)
    mlp = slice(3, None)
    token_block = tokens.reshape(2 * BLK, D)
    grad_block = cotangent.reshape(2 * BLK, D)

    small = jnp.concatenate([norm_gain, norm_shift, input_bias, output_bias])
    params = gather_small(small).astype(f32)
    cuts = [norm_gain.shape[0], norm_shift.shape[0], input_bias.shape[0], output_bias.shape[0]]
    ends = [sum(cuts[: k + 1]) for k in range(4)]
    gain, shift, bias_in, bias_out = (
        params[:, end - cut : end].reshape(-1) for cut, end in zip(cuts, ends)
    )

    x = gather_rows(token_block).astype(f32)
    weight_mlp = gather_dp(spread_columns(input_weight, mlp))
    weight_qkv = gather_dp(spread_columns(input_weight, qkv))
    weight_out = gather_dp(swap_units(output_weight, False))
    grads = gather_rows(grad_block)

    middle = jnp.mean(x, axis=-1, keepdims=True)
    centred = x - middle
    spread = jnp.mean(centred * centred, axis=-1, keepdims=True)
    xhat = centred * lax.rsqrt(spread + epsilon)
    normed = (xhat * gain + shift).astype(bf16)

    bias_columns = take_columns(bias_in[None], place, count, slice(None))
    hidden_mlp = dot(normed, weight_mlp, ((1,), (0,))) + bias_columns[:, 3 * own :]
    hidden_qkv = dot(normed, weight_qkv, ((1,), (0,))) + bias_columns[:, : 3 * own]
    activated, gelu_back = jax.vjp(lambda v: jax.nn.gelu(v, approximate=True), hidden_mlp)

    grad_mix = dot(grads, weight_out[:own], ((1,), (1,))).astype(bf16)
    grad_mlp = dot(grads, weight_out[own:], ((1,), (1,)))
    (grad_up,) = gelu_back(grad_mlp)
    grad_up = grad_up.astype(bf16)

    attended, grad_q, grad_k, grad_v = attention(hidden_qkv, grad_mix)
    grad_qkv = jnp.concatenate([grad_q, grad_k, grad_v], axis=1)
    branch = jnp.concatenate([attended, activated.astype(bf16)], axis=1)

    partial_out = dot(branch, weight_out, ((1,), (0,)))
    block_out = (
        (token_block.astype(f32) + scatter_rows(partial_out) + bias_out)
        .astype(bf16)
        .reshape(tokens.shape)
    )

    weight_out_term = dot(branch, grads, ((0,), (0,)))
    weightout_grad = swap_units(scatter_dp(weight_out_term).astype(bf16), True).astype(f32)

    weight_mlp_term = dot(normed, grad_up, ((0,), (0,)))
    weight_qkv_term = dot(normed, grad_qkv, ((0,), (0,)))
    weightin_grad = jnp.zeros(input_weight.shape, f32)
    weightin_grad = collect_columns(weightin_grad, scatter_dp(weight_mlp_term), mlp)
    weightin_grad = collect_columns(weightin_grad, scatter_dp(weight_qkv_term), qkv)

    grad_normed = dot(grad_qkv, weight_qkv, ((1,), (1,))) + dot(grad_up, weight_mlp, ((1,), (1,)))
    gain_term = jnp.sum(grad_normed * xhat, axis=0)
    shift_term = jnp.sum(grad_normed, axis=0)
    bias_in_term = jnp.concatenate(
        [jnp.sum(grad_qkv.astype(f32), axis=0), jnp.sum(grad_up.astype(f32), axis=0)]
    )
    bias_in_all = jnp.zeros((3 * D + FF,), f32)
    at = 0
    for start, width in column_pieces(place, count):
        bias_in_all = lax.dynamic_update_slice(bias_in_all, bias_in_term[at : at + width], (start,))
        at += width
    bias_out_term = jnp.sum(grad_block.astype(f32), axis=0)
    small_terms = jnp.concatenate(
        [
            gain_term.reshape(devices, -1),
            shift_term.reshape(devices, -1),
            bias_in_all.reshape(devices, -1),
            bias_out_term.reshape(devices, -1),
        ],
        axis=1,
    )
    small_grads = scatter_small(small_terms)
    gain_grad, shift_grad, biasin_grad, biasout_grad = (
        small_grads[end - cut : end] for cut, end in zip(cuts, ends)
    )

    own_normed = scatter_rows(grad_normed)
    own_x = token_block.astype(f32)
    own_centred = own_x - jnp.mean(own_x, axis=-1, keepdims=True)
    own_scale = lax.rsqrt(jnp.mean(own_centred * own_centred, axis=-1, keepdims=True) + epsilon)
    own_hat = own_centred * own_scale
    g = own_normed * gain
    tokens_grad = grad_block.astype(f32) + own_scale * (
        g
        - jnp.mean(g, axis=-1, keepdims=True)
        - own_hat * jnp.mean(g * own_hat, axis=-1, keepdims=True)
    )
    return (
        block_out,
        tokens_grad.reshape(tokens.shape),
        gain_grad,
        shift_grad,
        weightin_grad,
        biasin_grad,
        weightout_grad,
        biasout_grad,
    )


def solution(mesh):
    placed = (
        P("dp", None, "ctx", None, None),
        P(("dp", "ctx")),
        P(("dp", "ctx")),
        P(("dp", "ctx"), None),
        P(("dp", "ctx")),
        P(("dp", "ctx"), None),
        P(("dp", "ctx")),
        P("dp", None, "ctx", None, None),
    )
    return jax.shard_map(
        local,
        mesh=mesh,
        in_specs=placed,
        out_specs=(
            P("dp", None, "ctx", None, None),
            P("dp", None, "ctx", None, None),
            P(("dp", "ctx")),
            P(("dp", "ctx")),
            P(("dp", "ctx"), None),
            P(("dp", "ctx")),
            P(("dp", "ctx"), None),
            P(("dp", "ctx")),
        ),
        check_vma=False,
    )
```

```python
import functools
import math

import jax
import jax.numpy as jnp
from jax import lax
from jax.experimental import pallas as pl
from jax.experimental.pallas import tpu as pltpu
from jax.sharding import PartitionSpec as P

D = 2048
HEADS = 32
HEAD = 64
ROT = 32
BLK = 64
FF = 8192
TILE = 256

epsilon = 1e-05
theta_log = math.log(10000.0)
masked_fill = -1e30
bf16 = jnp.bfloat16
f32 = jnp.float32


def dot(a, b, dims):
    return lax.dot_general(a, b, (dims, ((), ())), preferred_element_type=f32)


def whole(shape, dtype):
    return jax.ShapeDtypeStruct(shape, dtype)


VMEM = pl.BlockSpec(memory_space=pltpu.VMEM)
SMEM = pl.BlockSpec(memory_space=pltpu.SMEM)
ROOM = pltpu.CompilerParams(vmem_limit_bytes=56 * 2**20)
LIGHT = pl.CostEstimate(flops=1, bytes_accessed=1, transcendentals=0)


def turn_lanes(values, cos, sin, sign):
    half = ROT // 2
    width = values.shape[-1]
    place = lax.broadcasted_iota(jnp.int32, (1, width), 1) % HEAD
    ahead = pltpu.roll(values, width - half, 1)
    behind = pltpu.roll(values, half, 1)
    turned = values * cos + sign * sin * jnp.where(place < half, -ahead, behind)
    return jnp.where(place < ROT, turned, values)


def head_scores(keys, q_head, start, reach, tile):
    scores = dot(keys, q_head, ((1,), (1,))) * 0.125
    allowed = lax.broadcasted_iota(jnp.int32, (reach, tile), 0) <= start + (
        lax.broadcasted_iota(jnp.int32, (reach, tile), 1)
    )
    return jnp.where(allowed, scores, masked_fill)


def for_row_tiles(length, tile, body):
    count = length // tile
    if count <= 4:
        for step in range(count):
            body(step * tile, (step + 1) * tile)
    else:
        per = count // 4
        for part in range(4):

            @pl.loop(part * per, (part + 1) * per)
            def _(step, part=part):
                body(pl.multiple_of(step * tile, tile), (part + 1) * per * tile)


def attention_kernel(length, width, stored, hq, hk, hv, gm, cos, sin, att, gq, gk, gv, qs, ks, vs, gs, kt, vt, raw, dk, dv):
    lanes = lax.broadcasted_iota(jnp.int32, (1, width), 1)
    tile = min(TILE, length)
    blocks = length // BLK
    cos_all, sin_all = cos[...], sin[...]

    def natural(ref, target):
        for b in range(blocks):
            target[b * BLK : (b + 1) * BLK, :] = ref[stored[b] : stored[b] + BLK, :]
        return target[...]

    qs[...] = turn_lanes(natural(hq, raw), cos_all, sin_all, 1.0).astype(bf16)
    keys_f32 = turn_lanes(natural(hk, raw), cos_all, sin_all, 1.0)
    ks[...] = keys_f32.astype(bf16)
    kt[...] = keys_f32.T.astype(bf16)
    values = natural(hv, raw)
    vs[...] = values.astype(bf16)
    vt[...] = values.T.astype(bf16)
    natural(gm, gs)
    dk[...] = jnp.zeros_like(dk)
    dv[...] = jnp.zeros_like(dv)

    def body(start, reach):
        rows = pl.ds(start, tile)
        q_rows = qs[rows, :]
        g_rows = gs[rows, :]
        keys = ks[0:reach, :]
        vals = vs[0:reach, :]
        mixes, gqs = [], []
        for head in range(width // HEAD):
            mine = (lanes // HEAD) == head
            q_head = jnp.where(mine, q_rows, jnp.zeros_like(q_rows))
            g_head = jnp.where(mine, g_rows, jnp.zeros_like(g_rows))
            span = slice(head * HEAD, (head + 1) * HEAD)
            scores = head_scores(keys, q_head, start, reach, tile)
            top = jnp.max(scores, axis=0, keepdims=True)
            weights = jnp.exp(scores - top)
            shares = weights * (1.0 / jnp.sum(weights, axis=0, keepdims=True))
            low = shares.astype(bf16)
            grad_shares = dot(vals, g_head, ((1,), (1,)))
            moved = shares * grad_shares
            inner = jnp.sum(moved, axis=0, keepdims=True)
            grad_scores = (moved - shares * inner).astype(bf16)
            mixes.append(dot(vt[span, 0:reach], low, ((1,), (0,))))
            gqs.append(dot(kt[span, 0:reach], grad_scores, ((1,), (0,))))
            dv[0:reach, :] += dot(low, g_head, ((1,), (0,)))
            dk[0:reach, :] += dot(grad_scores, q_head, ((1,), (0,)))
        raw[rows, :] = jnp.concatenate(mixes, axis=0).T
        grad_q = jnp.concatenate(gqs, axis=0).T * 0.125
        qs[rows, :] = turn_lanes(grad_q, cos[rows, :], sin[rows, :], -1.0).astype(bf16)

    for_row_tiles(length, tile, body)
    ks[...] = turn_lanes(dk[...] * 0.125, cos_all, sin_all, -1.0).astype(bf16)
    vs[...] = dv[...].astype(bf16)
    for b in range(blocks):
        here, there = slice(b * BLK, (b + 1) * BLK), slice(stored[b], stored[b] + BLK)
        att[there, :] = raw[here, :].astype(bf16)
        gq[there, :] = qs[here, :]
        gk[there, :] = ks[here, :]
        gv[there, :] = vs[here, :]


def rotary_tables(length, width):
    frequency = jnp.exp(-theta_log * 2.0 * jnp.arange(ROT // 2).astype(f32) / ROT)
    angles = jnp.arange(length, dtype=jnp.int32).astype(f32)[:, None] * frequency[None, :]
    spare = jnp.zeros((length, HEAD - ROT), f32)
    repeat = width // HEAD
    cos = jnp.tile(jnp.concatenate([jnp.cos(angles)] * 2 + [spare], axis=1), (1, repeat))
    sin = jnp.tile(jnp.concatenate([jnp.sin(angles)] * 2 + [spare], axis=1), (1, repeat))
    return cos, sin


def attention(hidden, grad_mix, stored, tables):
    length, columns = grad_mix.shape
    width = min(128, columns)
    groups = columns // width
    group = pl.BlockSpec((length, width), lambda g: (0, g))
    table = pl.BlockSpec((length, width), lambda g: (0, 0))
    if width < 128:
        parts = [hidden[:, k * columns : (k + 1) * columns] for k in range(3)]
        specs = [group] * 3
    else:
        parts = [hidden] * 3
        specs = [pl.BlockSpec((length, width), lambda g, k=k: (0, k * groups + g)) for k in range(3)]
    return pl.pallas_call(
        functools.partial(attention_kernel, length, width, stored),
        grid=(groups,),
        in_specs=specs + [group, table, table],
        out_specs=[group] * 4,
        out_shape=[whole((length, columns), bf16)] * 4,
        scratch_shapes=[pltpu.VMEM((length, width), bf16)] * 4
        + [pltpu.VMEM((width, length), bf16)] * 2
        + [pltpu.VMEM((length, width), f32)] * 3,
        compiler_params=ROOM,
        cost_estimate=LIGHT,
        name="attention",
    )(*parts, grad_mix, *tables)


def norm_kernel(owners, gain, shift, *refs):
    blocks, (normed, hats) = refs[:-2], refs[-2:]
    rows = blocks[0].shape[0]
    for b, ref in enumerate(blocks):
        x = ref[...].astype(f32)
        centred = x - jnp.mean(x, axis=-1, keepdims=True)
        hat = centred * lax.rsqrt(jnp.mean(centred * centred, axis=-1, keepdims=True) + epsilon)
        there = pl.ds(pl.multiple_of(owners[b] * rows, rows), rows)
        normed[there, :] = (hat * gain[...] + shift[...]).astype(bf16)
        hats[there, :] = hat.astype(bf16)


def norm_blocks(blocks, owners, gain, shift):
    rows = blocks[0].shape[0]
    total = rows * len(blocks)
    if total > 1024:
        normed = hats = jnp.zeros((total, D), bf16)
        for b, block in enumerate(blocks):
            x = block.astype(f32)
            centred = x - jnp.mean(x, axis=-1, keepdims=True)
            spread = jnp.mean(centred * centred, axis=-1, keepdims=True)
            hat = centred * lax.rsqrt(spread + epsilon)
            at = (owners[b] * rows, 0)
            normed = lax.dynamic_update_slice(normed, (hat * gain + shift).astype(bf16), at)
            hats = lax.dynamic_update_slice(hats, hat.astype(bf16), at)
        return normed, hats
    return pl.pallas_call(
        norm_kernel,
        in_specs=[SMEM] + [VMEM] * (2 + len(blocks)),
        out_specs=[VMEM] * 2,
        out_shape=[whole((total, D), bf16)] * 2,
        compiler_params=ROOM,
        cost_estimate=LIGHT,
        name="norm",
    )(owners, gain[None], shift[None], *blocks)


def order_kernel(owners, *refs):
    *blocks, out = refs
    rows = blocks[0].shape[0]
    for b, ref in enumerate(blocks):
        out[pl.ds(pl.multiple_of(owners[b] * rows, rows), rows), :] = ref[...]


def order_blocks(blocks, owners):
    rows, columns = blocks[0].shape
    return pl.pallas_call(
        order_kernel,
        in_specs=[SMEM] + [VMEM] * len(blocks),
        out_specs=VMEM,
        out_shape=whole((rows * len(blocks), columns), blocks[0].dtype),
        compiler_params=ROOM,
        cost_estimate=LIGHT,
        name="order_blocks",
    )(owners, *blocks)


def column_pieces(index, count):
    own = D // count
    rows = (D + FF) // (4 * count)
    pieces = [(which * D + index * own, own) for which in range(3)]
    pieces.append((3 * D + index * (rows - own), rows - own))
    for part in range(1, 4):
        pieces.append((3 * D + part * rows * count - D + index * rows, rows))
    return pieces


def split_kernel(count, weight, out):
    for index in range(count):
        at = 0
        for start, width in column_pieces(index, count):
            out[index, :, at : at + width] = weight[:, start : start + width]
            at += width


def split_columns(weight, count):
    rows, columns = weight.shape
    return pl.pallas_call(
        functools.partial(split_kernel, count),
        in_specs=[VMEM],
        out_specs=VMEM,
        out_shape=whole((count, rows, columns // count), weight.dtype),
        compiler_params=ROOM,
        cost_estimate=LIGHT,
        name="split_columns",
    )(weight)


def join_kernel(count, spans, *refs):
    *splits, out = refs
    for split, span in zip(splits, spans):
        for index in range(count):
            at = 0
            for start, width in column_pieces(index, count)[span]:
                out[:, start : start + width] = split[index, :, at : at + width].astype(f32)
                at += width


def join_columns(splits, spans, count):
    rows = splits[0].shape[1]
    return pl.pallas_call(
        functools.partial(join_kernel, count, spans),
        in_specs=[VMEM] * len(splits),
        out_specs=VMEM,
        out_shape=whole((rows, 3 * D + FF), f32),
        compiler_params=ROOM,
        cost_estimate=LIGHT,
        name="join_columns",
    )(*splits)


def product_kernel(number, owners, *refs):
    parts, (weight, hats), (*outs, sums) = refs[:number], refs[number : number + 2], refs[number + 2 :]
    rows = outs[0].shape[0]
    half = len(outs) // 2
    gain = shift = 0.0
    for low in (half, 0):
        there = [
            pl.ds(pl.multiple_of(owners[low + k] * rows, rows), rows) for k in range(half)
        ]
        total, at = None, 0
        for part in parts:
            size = part.shape[1]
            taken = jnp.concatenate([part[rows_k, :] for rows_k in there])
            term = dot(taken, weight[:, at : at + size], ((1,), (1,)))
            total = term if total is None else total + term
            at += size
        hat = jnp.concatenate([hats[rows_k, :] for rows_k in there]).astype(f32)
        gain += jnp.sum(total * hat, axis=0, keepdims=True)
        shift += jnp.sum(total, axis=0, keepdims=True)
        for k in range(half):
            out = outs[low + k]
            out[...] = total[k * rows : (k + 1) * rows].astype(out.dtype)
    sums[0:1, :] = gain
    sums[1:2, :] = shift


def product_blocks(parts, weight, hats, owners, count):
    rows = parts[0].shape[0] // count
    depth = sum(part.shape[1] for part in parts)
    tile = D // 4
    return pl.pallas_call(
        functools.partial(product_kernel, len(parts)),
        grid_spec=pltpu.PrefetchScalarGridSpec(
            num_scalar_prefetch=1,
            grid=(D // tile,),
            in_specs=[pl.BlockSpec(part.shape, lambda n, *_: (0, 0)) for part in parts]
            + [
                pl.BlockSpec((tile, depth), lambda n, *_: (n, 0)),
                pl.BlockSpec((rows * count, tile), lambda n, *_: (0, n)),
            ],
            out_specs=[pl.BlockSpec((rows, tile), lambda n, *_: (0, n))] * count
            + [pl.BlockSpec((8, tile), lambda n, *_: (0, n))],
        ),
        out_shape=[whole((rows, D), f32)] * (count // 2)
        + [whole((rows, D), bf16)] * (count // 2)
        + [whole((8, D), f32)],
        compiler_params=ROOM,
        cost_estimate=LIGHT,
        name="product_blocks",
    )(owners, *parts, weight, hats)


def after(value, *others):
    return lax.optimization_barrier((value, *others))[0]


class Rounds:
    def __init__(self):
        self.token = ()

    def begin(self, *values):
        tied = lax.optimization_barrier((*values, *self.token))
        return tied[0] if len(values) == 1 else tied[: len(values)]

    def end(self, *values):
        self.token = lax.optimization_barrier(values)
        return self.token


def shift_pairs(size, by):
    return [(k, (k + by) % size) for k in range(size)]


def flip_pairs(size, bit):
    return [(k, k ^ bit) for k in range(size)]


def to_y(value):
    return lax.ppermute(value, "ctx", flip_pairs(lax.axis_size("ctx"), 1))


def to_z(value, by):
    return lax.ppermute(value, "ctx", shift_pairs(lax.axis_size("ctx"), 2 * by))


def to_x(value):
    return lax.ppermute(value, "dp", flip_pairs(4, 2))


def to_core(value):
    return lax.ppermute(value, "dp", flip_pairs(4, 1))


def small_steps():
    steps = []
    for axis in ("ctx", "dp"):
        bit = 1
        while bit < lax.axis_size(axis):
            steps.append((axis, bit, (lax.axis_index(axis) & bit) != 0))
            bit *= 2
    return steps


def swap(value, axis, bit):
    return lax.ppermute(value, axis, flip_pairs(lax.axis_size(axis), bit))


def halve(held, upper):
    half = held.shape[0] // 2
    low, high = held[:half], held[half:]
    return jnp.where(upper, low, high), jnp.where(upper, high, low)


def unit_rounds(count):
    edges = []
    for m in range(5 * count):
        owner, slot = (m // 4, m % 4) if m < 4 * count else (m - 4 * count, 4)
        edges.append((m // 5, m % 5, owner, slot))
    rounds = []
    left = list(edges)
    for _ in range(5):
        by_source = [[e for e in left if e[0] == s] for s in range(count)]
        taken = {}

        def place_edge(source, seen):
            for edge in by_source[source]:
                if edge[2] in seen:
                    continue
                seen.add(edge[2])
                if edge[2] not in taken or place_edge(taken[edge[2]][0], seen):
                    taken[edge[2]] = edge
                    return True
            return False

        for source in range(count):
            assert place_edge(source, set())
        chosen = {edge[0]: edge for edge in taken.values()}
        rounds.append([chosen[s] for s in range(count)])
        for edge in taken.values():
            left.remove(edge)
    return rounds


def unit_table(count, back):
    table, rounds = [[0] * 10 for _ in range(count)], []
    for turn, chosen in enumerate(unit_rounds(count)):
        pairs = []
        for source, unit, owner, slot in chosen:
            if back:
                source, unit, owner, slot = owner, slot, source, unit
            pairs.append((source, owner))
            table[source][turn] = unit
            table[owner][5 + turn] = slot
        rounds.append(pairs)
    return jnp.array(table, jnp.int32), rounds


def unit_out_kernel(units, block, *outs):
    rows = outs[0].shape[0]
    for turn, out in enumerate(outs):
        out[...] = block[pl.ds(pl.multiple_of(units[turn] * rows, rows), rows), :]


def unit_in_kernel(units, first, block, *refs):
    *gots, out = refs
    rows = gots[0].shape[0]

    @pl.when(first[0] == 1)
    def _():
        for turn, got in enumerate(gots):
            at = pl.multiple_of(units[5 + turn] * rows, rows)
            out[pl.ds(at, rows), :] = got[...].astype(out.dtype)

    @pl.when(first[0] == 0)
    def _():
        out[...] = block[...].astype(out.dtype)


class Units:
    def __init__(self, back, first):
        self.count = lax.axis_size("ctx")
        table, self.rounds = unit_table(self.count, back)
        self.units = table[lax.axis_index("ctx")]
        self.first = first.astype(jnp.int32)[None]

    def split(self, block):
        rows, columns = block.shape
        return pl.pallas_call(
            unit_out_kernel,
            in_specs=[SMEM, VMEM],
            out_specs=[VMEM] * 5,
            out_shape=[whole((rows // 5, columns), bf16)] * 5,
            compiler_params=ROOM,
            cost_estimate=LIGHT,
            name="unit_out",
        )(self.units, block)

    def send(self, parts, turn):
        return lax.ppermute(parts[turn], "ctx", self.rounds[turn])

    def merge(self, block, got, dtype):
        return pl.pallas_call(
            unit_in_kernel,
            in_specs=[SMEM, SMEM] + [VMEM] * 6,
            out_specs=VMEM,
            out_shape=whole(block.shape, dtype),
            compiler_params=ROOM,
            cost_estimate=LIGHT,
            name="unit_in",
        )(self.units, self.first, block, *got)


def local(
    tokens, norm_gain, norm_shift, input_weight, input_bias, output_weight, output_bias, cotangent
):
    count = lax.axis_size("ctx")
    place = lax.axis_index("ctx")
    dp_place = lax.axis_index("dp")
    far = count // 2
    z, y = place // 2, place % 2
    devices = 4 * count
    own = D // count
    length = 2 * BLK * count
    rows_out = output_weight.shape[0]
    token_block = tokens.reshape(2 * BLK, D)
    grad_block = cotangent.reshape(2 * BLK, D)

    stored = [min(b, 2 * count - 1 - b) * 2 * BLK + BLK * (b >= count) for b in range(2 * count)]
    steps = jnp.arange(far, dtype=jnp.int32)
    owners_mine = ((z + far - steps) % far) * 2 + y
    owners = jnp.concatenate([owners_mine, owners_mine ^ 1])
    tables = rotary_tables(length, min(128, own))
    rounds = Rounds()
    gather = lambda v, axis: lax.all_gather(v, axis, axis=0, tiled=True)
    scatter = lambda v, axis: lax.psum_scatter(v, axis, scatter_dimension=0, tiled=True)

    small = jnp.concatenate([norm_gain, norm_shift, input_bias, output_bias])
    cuts = [norm_gain.shape[0], norm_shift.shape[0], input_bias.shape[0], output_bias.shape[0]]
    ends = [sum(cuts[: k + 1]) for k in range(4)]
    out_raw = gather(output_weight, "dp")
    packed = split_columns(input_weight, count)
    held, other = [token_block, to_z(token_block, 1)], [to_y(token_block)]
    columns = lax.all_to_all(packed, "ctx", 0, 0, tiled=True)
    vectors = after(small[None], packed)
    for axis, bit, upper in small_steps():
        got = swap(vectors, axis, bit)
        vectors = jnp.where(
            upper, jnp.concatenate([got, vectors]), jnp.concatenate([vectors, got])
        )
    held[1], other[0], columns, vectors = rounds.end(held[1], other[0], columns, vectors)
    weight_in = gather(columns.reshape(-1, columns.shape[-1]), "dp")
    gain, shift, bias_in, bias_out = (
        vectors[:, end - cut : end].reshape(-1).astype(f32) for cut, end in zip(cuts, ends)
    )
    bias_own = jnp.concatenate(
        [lax.dynamic_slice_in_dim(bias_in, start, width) for start, width in column_pieces(place, count)]
    )

    units = Units(False, dp_place >= 0)
    unit_parts = units.split(rounds.begin(out_raw)[:rows_out])
    unit_got = []
    grad_held, grad_other = [grad_block], []
    for step in range(1, far):
        last = step == far - 1
        source = rounds.begin(held[step])
        started = [to_y(source), to_z(rounds.begin(grad_block), 1) if last else to_z(source, 1)]
        turns = range(len(unit_got), 5 if last else min(5, len(unit_got) + 2))
        started += [units.send(unit_parts, turn) for turn in turns]
        started = list(rounds.end(*started))
        other.append(started[0])
        (grad_held if last else held).append(started[1])
        unit_got += started[2:]

    gelu = lambda v: jax.nn.gelu(v, approximate=True)
    normed = hats = hidden = activated = hidden_qkv = None
    for step in range(far):
        source = rounds.begin(grad_held[step])
        started = [to_y(source)]
        if 0 < step < far - 1:
            started.append(to_z(source, 1))
        sends = len(started)
        if step == 0:
            normed, hats = norm_blocks(rounds.begin(*held, *other), owners, gain, shift)
            rest = [normed, hats]
        elif step == 1:
            hidden = dot(rounds.begin(normed), weight_in[:, 3 * own :], ((1,), (0,))) + bias_own[3 * own :]
            activated = gelu(hidden).astype(bf16)
            rest = [hidden, activated]
        elif step == 2:
            hidden_qkv = (
                dot(rounds.begin(normed), weight_in[:, : 3 * own], ((1,), (0,))) + bias_own[: 3 * own]
            )
            weight_out = lax.dynamic_update_slice(
                out_raw, units.merge(out_raw[:rows_out], unit_got, bf16), (0, 0)
            )
            rest = [hidden_qkv]
        else:
            rest = []
        started = rounds.end(*started, *rest)
        if step == 0:
            normed, hats = started[sends:]
        elif step == 1:
            hidden, activated = started[sends:]
        elif step == 2:
            hidden_qkv = started[sends]
        grad_other.append(started[0])
        grad_held += started[1:sends]
    grads = order_blocks(rounds.begin(*grad_held, *grad_other), owners)

    part = D // 4
    near = lambda r: lax.dynamic_slice_in_dim(normed, (dp_place ^ r) * part, part, 1)
    term = lambda r, chunk: dot(near(r), chunk, ((0,), (0,)))
    far_terms = lambda chunk: jnp.concatenate([term(1, chunk), term(3, chunk)]).astype(bf16)
    mid_terms = lambda chunk, got: (term(2, chunk) + got[part:].astype(f32)).astype(bf16)

    def near_terms(chunk, got, across):
        total = term(0, chunk) + got[:part].astype(f32) + across.astype(f32)
        return total.astype(bf16).reshape(count, part // count, -1)

    spread = lambda v: lax.all_to_all(v, "ctx", 0, 0, tiled=True)
    (grad_up,) = jax.vjp(gelu, hidden)[1](dot(grads, weight_out[own:], ((1,), (1,))))
    grad_up = grad_up.astype(bf16)
    beside = to_core(far_terms(grad_up))
    grad_mix = dot(grads, weight_out[:own], ((1,), (1,))).astype(bf16)
    beside, grad_mix = rounds.end(beside, grad_mix)
    across = to_x(mid_terms(grad_up, beside))
    attended, *grad_qkv = attention(rounds.begin(hidden_qkv), grad_mix, stored, tables)
    across, attended, *grad_qkv = rounds.end(across, attended, *grad_qkv)
    came_mlp = spread(near_terms(grad_up, beside, across))
    branch = jnp.concatenate([attended, activated], axis=1)
    out_term = dot(branch, grads, ((0,), (0,))).astype(bf16)
    out_own = scatter(out_term, "dp")
    *normed_terms, sums = product_blocks(
        [*after(tuple(grad_qkv), out_term), grad_up], weight_in, hats, owners, count
    )
    out_part = dot(after(branch, sums), weight_out, ((1,), (0,))).astype(bf16)
    out_sum = scatter(out_part, "ctx")
    grad_heads = jnp.concatenate(grad_qkv, axis=1)
    sent_heads = far_terms(grad_heads)
    came_mlp, sums, sent_heads, *normed_terms = rounds.end(came_mlp, sums, sent_heads, *normed_terms)

    bias_terms = [jnp.sum(v.astype(f32), axis=0) for v in grad_qkv]
    up_terms, at = jnp.sum(grad_up.astype(f32), axis=0), 0
    for _, width in column_pieces(0, count)[3:]:
        bias_terms.append(up_terms[at : at + width])
        at += width
    here = (jnp.arange(count) == place).astype(f32)[:, None]
    vector_terms = jnp.concatenate(
        [
            sums[0].reshape(devices, -1),
            sums[1].reshape(devices, -1),
            jnp.concatenate([(here * t[None]).reshape(-1) for t in bias_terms]).reshape(devices, -1),
            jnp.sum(grad_block.astype(f32), axis=0).reshape(devices, -1),
        ],
        axis=1,
    )
    small_left = small_steps()[::-1]

    def small_step(terms):
        axis, bit, upper = small_left.pop(0)
        give, keep = halve(terms, upper)
        return swap(give, axis, bit), keep

    mine, theirs = normed_terms[:far], normed_terms[far:]
    got, running = [None] * far, None
    back = Units(True, dp_place == 0)
    back_parts, back_got = None, []
    left_y, left_z, stage = list(range(far))[::-1], list(range(1, far))[::-1], 0
    beside = across = came_heads = None
    while left_y or left_z or stage < 4:
        names, started = [], []

        def start(name, value):
            names.append(name)
            started.append(value)

        z_now = left_z[0] if left_z and got[left_z[0]] is not None else None
        pair = left_y[:2]
        left_y = left_y[2:]
        for k in pair:
            start(("y", k), to_y(rounds.begin(theirs[k])))
        if z_now is not None:
            left_z.pop(0)
            joint = mine[z_now] + got[z_now].astype(f32)
            if running is not None:
                joint = joint + running.astype(f32)
            start("z", to_z(rounds.begin(joint.astype(bf16)), -1))
        if stage == 0:
            start("core", to_core(rounds.begin(sent_heads)))
        elif stage == 1:
            start("x", to_x(rounds.begin(mid_terms(grad_heads, beside))))
        elif stage == 2:
            start("spread", spread(rounds.begin(near_terms(grad_heads, beside, across))))
        if stage >= 2 and len(back_got) < 5:
            if back_parts is None:
                back_parts = back.split(rounds.begin(out_own))
            for turn in range(len(back_got), min(5, len(back_got) + 3)):
                start("unit", back.send(back_parts, turn))
        if small_left:
            give, keep = small_step(rounds.begin(vector_terms))
            start("give", give)
            start("keep", keep)
        stage += 1
        for name, value in zip(names, rounds.end(*started)):
            if name == "z":
                running = value
            elif name == "core":
                beside = value
            elif name == "x":
                across = value
            elif name == "spread":
                came_heads = value
            elif name == "unit":
                back_got.append(value)
            elif name == "give":
                vector_terms = value
            elif name == "keep":
                vector_terms = vector_terms + value
            else:
                got[name[1]] = value
    joined = lambda step: mine[step] + got[step].astype(f32)
    weightin_grad = join_columns([came_heads, came_mlp], [slice(0, 3), slice(3, None)], count)
    weightout_grad = back.merge(out_own, back_got, f32)
    while small_left:
        give, keep = small_step(vector_terms)
        vector_terms = give + keep
    gain_grad, shift_grad, biasin_grad, biasout_grad = (
        vector_terms[0, end - cut : end] for cut, end in zip(cuts, ends)
    )

    own_normed = joined(0) + running.astype(f32)
    own_x = token_block.astype(f32)
    centred = own_x - jnp.mean(own_x, axis=-1, keepdims=True)
    scale = lax.rsqrt(jnp.mean(centred * centred, axis=-1, keepdims=True) + epsilon)
    hat = centred * scale
    g = own_normed * gain
    tokens_grad = grad_block.astype(f32) + scale * (
        g - jnp.mean(g, axis=-1, keepdims=True) - hat * jnp.mean(g * hat, axis=-1, keepdims=True)
    )
    block_out = (token_block.astype(f32) + out_sum.astype(f32) + bias_out).astype(bf16)
    return (
        block_out.reshape(tokens.shape),
        tokens_grad.reshape(tokens.shape),
        gain_grad,
        shift_grad,
        weightin_grad,
        biasin_grad,
        weightout_grad,
        biasout_grad,
    )


def solution(mesh):
    placed = (
        P("dp", None, "ctx", None, None),
        P(("dp", "ctx")),
        P(("dp", "ctx")),
        P(("dp", "ctx"), None),
        P(("dp", "ctx")),
        P(("dp", "ctx"), None),
        P(("dp", "ctx")),
        P("dp", None, "ctx", None, None),
    )
    return jax.shard_map(
        local,
        mesh=mesh,
        in_specs=placed,
        out_specs=(
            P("dp", None, "ctx", None, None),
            P("dp", None, "ctx", None, None),
            P(("dp", "ctx")),
            P(("dp", "ctx")),
            P(("dp", "ctx"), None),
            P(("dp", "ctx")),
            P(("dp", "ctx"), None),
            P(("dp", "ctx")),
        ),
        check_vma=False,
    )
```

```python
import functools
import math

import jax
import jax.numpy as jnp
from jax import lax
from jax.experimental import pallas as pl
from jax.experimental.pallas import tpu as pltpu
from jax.sharding import PartitionSpec as P

D = 2048
HEADS = 32
HEAD = 64
ROT = 32
BLK = 64
FF = 8192
TILE = 256

epsilon = 1e-05
theta_log = math.log(10000.0)
masked_fill = -1e30
bf16 = jnp.bfloat16
f32 = jnp.float32


def dot(a, b, dims):
    return lax.dot_general(a, b, (dims, ((), ())), preferred_element_type=f32)


def whole(shape, dtype):
    return jax.ShapeDtypeStruct(shape, dtype)


VMEM = pl.BlockSpec(memory_space=pltpu.VMEM)
SMEM = pl.BlockSpec(memory_space=pltpu.SMEM)
ROOM = pltpu.CompilerParams(vmem_limit_bytes=56 * 2**20)
LIGHT = pl.CostEstimate(flops=1, bytes_accessed=1, transcendentals=0)


def turn_lanes(values, cos, sin, sign):
    half = ROT // 2
    width = values.shape[-1]
    place = lax.broadcasted_iota(jnp.int32, (1, width), 1) % HEAD
    ahead = pltpu.roll(values, width - half, 1)
    behind = pltpu.roll(values, half, 1)
    turned = values * cos + sign * sin * jnp.where(place < half, -ahead, behind)
    return jnp.where(place < ROT, turned, values)


def head_scores(keys, q_head, start, reach, tile):
    scores = dot(keys, q_head, ((1,), (1,))) * 0.125
    allowed = lax.broadcasted_iota(jnp.int32, (reach, tile), 0) <= start + (
        lax.broadcasted_iota(jnp.int32, (reach, tile), 1)
    )
    return jnp.where(allowed, scores, masked_fill)


def for_row_tiles(length, tile, body):
    count = length // tile
    if count <= 4:
        for step in range(count):
            body(step * tile, (step + 1) * tile)
    else:
        per = count // 4
        for part in range(4):

            @pl.loop(part * per, (part + 1) * per)
            def _(step, part=part):
                body(pl.multiple_of(step * tile, tile), (part + 1) * per * tile)


def forward_kernel(length, width, stored, hq, hk, hv, cos, sin, att, qs, ks, vs, stats, raw, vt):
    lanes = lax.broadcasted_iota(jnp.int32, (1, width), 1)
    tile = min(TILE, length)
    blocks = length // BLK
    cos_all, sin_all = cos[...], sin[...]

    def natural(ref):
        for b in range(blocks):
            raw[b * BLK : (b + 1) * BLK, :] = ref[stored[b] : stored[b] + BLK, :]
        return raw[...]

    qs[...] = turn_lanes(natural(hq), cos_all, sin_all, 1.0).astype(bf16)
    ks[...] = turn_lanes(natural(hk), cos_all, sin_all, 1.0).astype(bf16)
    values = natural(hv)
    vs[...] = values.astype(bf16)
    vt[...] = values.T.astype(bf16)

    def body(start, reach):
        rows = pl.ds(start, tile)
        q_rows = qs[rows, :]
        keys = ks[0:reach, :]
        mixes = []
        for head in range(width // HEAD):
            mine = (lanes // HEAD) == head
            q_head = jnp.where(mine, q_rows, jnp.zeros_like(q_rows))
            scores = head_scores(keys, q_head, start, reach, tile)
            top = jnp.max(scores, axis=0, keepdims=True)
            weights = jnp.exp(scores - top)
            part = 1.0 / jnp.sum(weights, axis=0, keepdims=True)
            stats[0, 2 * head : 2 * head + 1, rows] = top
            stats[0, 2 * head + 1 : 2 * head + 2, rows] = part
            low = (weights * part).astype(bf16)
            mixes.append(dot(vt[head * HEAD : (head + 1) * HEAD, 0:reach], low, ((1,), (0,))))
        raw[rows, :] = jnp.concatenate(mixes, axis=0).T

    for_row_tiles(length, tile, body)
    for b in range(blocks):
        att[stored[b] : stored[b] + BLK, :] = raw[b * BLK : (b + 1) * BLK, :].astype(bf16)


def backward_kernel(length, width, stored, qs, ks, vs, stats, gm, cos, sin, gq, gk, gv, gs, kt, dq, dk, dv):
    lanes = lax.broadcasted_iota(jnp.int32, (1, width), 1)
    tile = min(TILE, length)
    blocks = length // BLK
    for b in range(blocks):
        gs[b * BLK : (b + 1) * BLK, :] = gm[stored[b] : stored[b] + BLK, :]
    kt[...] = ks[...].T
    dk[...] = jnp.zeros_like(dk)
    dv[...] = jnp.zeros_like(dv)

    def body(start, reach):
        rows = pl.ds(start, tile)
        q_rows = qs[rows, :]
        g_rows = gs[rows, :]
        keys = ks[0:reach, :]
        vals = vs[0:reach, :]
        gqs = []
        for head in range(width // HEAD):
            mine = (lanes // HEAD) == head
            q_head = jnp.where(mine, q_rows, jnp.zeros_like(q_rows))
            g_head = jnp.where(mine, g_rows, jnp.zeros_like(g_rows))
            scores = head_scores(keys, q_head, start, reach, tile)
            top = stats[0, 2 * head : 2 * head + 1, rows]
            part = stats[0, 2 * head + 1 : 2 * head + 2, rows]
            shares = jnp.exp(scores - top) * part
            grad_shares = dot(vals, g_head, ((1,), (1,)))
            moved = shares * grad_shares
            inner = jnp.sum(moved, axis=0, keepdims=True)
            grad_scores = (moved - shares * inner).astype(bf16)
            gqs.append(dot(kt[head * HEAD : (head + 1) * HEAD, 0:reach], grad_scores, ((1,), (0,))))
            dv[0:reach, :] += dot(shares.astype(bf16), g_head, ((1,), (0,)))
            dk[0:reach, :] += dot(grad_scores, q_head, ((1,), (0,)))
        grad_q = jnp.concatenate(gqs, axis=0).T * 0.125
        dq[rows, :] = turn_lanes(grad_q, cos[rows, :], sin[rows, :], -1.0).astype(bf16)

    for_row_tiles(length, tile, body)
    grad_k = turn_lanes(dk[...] * 0.125, cos[...], sin[...], -1.0).astype(bf16)
    grad_v = dv[...].astype(bf16)
    for b in range(blocks):
        here, there = slice(b * BLK, (b + 1) * BLK), slice(stored[b], stored[b] + BLK)
        gq[there, :] = dq[here, :]
        gk[there, :] = grad_k[here]
        gv[there, :] = grad_v[here]


def rotary_tables(length, width):
    frequency = jnp.exp(-theta_log * 2.0 * jnp.arange(ROT // 2).astype(f32) / ROT)
    angles = jnp.arange(length, dtype=jnp.int32).astype(f32)[:, None] * frequency[None, :]
    spare = jnp.zeros((length, HEAD - ROT), f32)
    repeat = width // HEAD
    cos = jnp.tile(jnp.concatenate([jnp.cos(angles)] * 2 + [spare], axis=1), (1, repeat))
    sin = jnp.tile(jnp.concatenate([jnp.sin(angles)] * 2 + [spare], axis=1), (1, repeat))
    return cos, sin


def attention_specs(length, columns):
    width = min(128, columns)
    groups = columns // width
    group = pl.BlockSpec((length, width), lambda g: (0, g))
    table = pl.BlockSpec((length, width), lambda g: (0, 0))
    stats = pl.BlockSpec((1, 8, length), lambda g: (g, 0, 0))
    return width, groups, group, table, stats


def attention_forward(hidden, columns, stored, tables):
    length = hidden.shape[0]
    width, groups, group, table, stats = attention_specs(length, columns)
    if width < 128:
        parts = [hidden[:, k * columns : (k + 1) * columns] for k in range(3)]
        specs = [group] * 3
    else:
        parts = [hidden] * 3
        specs = [pl.BlockSpec((length, width), lambda g, k=k: (0, k * groups + g)) for k in range(3)]
    return pl.pallas_call(
        functools.partial(forward_kernel, length, width, stored),
        grid=(groups,),
        in_specs=specs + [table, table],
        out_specs=[group] * 4 + [stats],
        out_shape=[whole((length, columns), bf16)] * 4 + [whole((groups, 8, length), f32)],
        scratch_shapes=[pltpu.VMEM((length, width), f32), pltpu.VMEM((width, length), bf16)],
        compiler_params=ROOM,
        cost_estimate=LIGHT,
        name="attention_forward",
    )(*parts, *tables)


def attention_backward(kept, grad_mix, stored, tables):
    length, columns = grad_mix.shape
    width, groups, group, table, stats = attention_specs(length, columns)
    return pl.pallas_call(
        functools.partial(backward_kernel, length, width, stored),
        grid=(groups,),
        in_specs=[group] * 3 + [stats, group, table, table],
        out_specs=[group] * 3,
        out_shape=[whole((length, columns), bf16)] * 3,
        scratch_shapes=[
            pltpu.VMEM((length, width), bf16),
            pltpu.VMEM((width, length), bf16),
            pltpu.VMEM((length, width), bf16),
            pltpu.VMEM((length, width), f32),
            pltpu.VMEM((length, width), f32),
        ],
        compiler_params=ROOM,
        cost_estimate=LIGHT,
        name="attention_backward",
    )(*kept, grad_mix, *tables)


def norm_kernel(owners, gain, shift, *refs):
    blocks, (normed, hats) = refs[:-2], refs[-2:]
    rows = blocks[0].shape[0]
    for b, ref in enumerate(blocks):
        x = ref[...].astype(f32)
        centred = x - jnp.mean(x, axis=-1, keepdims=True)
        hat = centred * lax.rsqrt(jnp.mean(centred * centred, axis=-1, keepdims=True) + epsilon)
        there = pl.ds(pl.multiple_of(owners[b] * rows, rows), rows)
        normed[there, :] = (hat * gain[...] + shift[...]).astype(bf16)
        hats[there, :] = hat.astype(bf16)


def norm_blocks(blocks, owners, gain, shift):
    rows = blocks[0].shape[0]
    total = rows * len(blocks)
    if total > 1024:
        normed = hats = jnp.zeros((total, D), bf16)
        for b, block in enumerate(blocks):
            x = block.astype(f32)
            centred = x - jnp.mean(x, axis=-1, keepdims=True)
            spread = jnp.mean(centred * centred, axis=-1, keepdims=True)
            hat = centred * lax.rsqrt(spread + epsilon)
            at = (owners[b] * rows, 0)
            normed = lax.dynamic_update_slice(normed, (hat * gain + shift).astype(bf16), at)
            hats = lax.dynamic_update_slice(hats, hat.astype(bf16), at)
        return normed, hats
    return pl.pallas_call(
        norm_kernel,
        in_specs=[SMEM] + [VMEM] * (2 + len(blocks)),
        out_specs=[VMEM] * 2,
        out_shape=[whole((total, D), bf16)] * 2,
        compiler_params=ROOM,
        cost_estimate=LIGHT,
        name="norm",
    )(owners, gain[None], shift[None], *blocks)


def order_kernel(owners, *refs):
    *blocks, out = refs
    rows = blocks[0].shape[0]
    for b, ref in enumerate(blocks):
        out[pl.ds(pl.multiple_of(owners[b] * rows, rows), rows), :] = ref[...]


def order_blocks(blocks, owners):
    rows, columns = blocks[0].shape
    return pl.pallas_call(
        order_kernel,
        in_specs=[SMEM] + [VMEM] * len(blocks),
        out_specs=VMEM,
        out_shape=whole((rows * len(blocks), columns), blocks[0].dtype),
        compiler_params=ROOM,
        cost_estimate=LIGHT,
        name="order_blocks",
    )(owners, *blocks)


def column_pieces(index, count):
    own = D // count
    rows = (D + FF) // (4 * count)
    pieces = [(which * D + index * own, own) for which in range(3)]
    pieces.append((3 * D + index * (rows - own), rows - own))
    for part in range(1, 4):
        pieces.append((3 * D + part * rows * count - D + index * rows, rows))
    return pieces


def split_kernel(count, weight, out):
    for index in range(count):
        at = 0
        for start, width in column_pieces(index, count):
            out[index, :, at : at + width] = weight[:, start : start + width]
            at += width


def split_columns(weight, count):
    rows, columns = weight.shape
    return pl.pallas_call(
        functools.partial(split_kernel, count),
        in_specs=[VMEM],
        out_specs=VMEM,
        out_shape=whole((count, rows, columns // count), weight.dtype),
        compiler_params=ROOM,
        cost_estimate=LIGHT,
        name="split_columns",
    )(weight)


def join_kernel(count, spans, *refs):
    *splits, out = refs
    for split, span in zip(splits, spans):
        for index in range(count):
            at = 0
            for start, width in column_pieces(index, count)[span]:
                out[:, start : start + width] = split[index, :, at : at + width].astype(f32)
                at += width


def join_columns(splits, spans, count):
    rows = splits[0].shape[1]
    return pl.pallas_call(
        functools.partial(join_kernel, count, spans),
        in_specs=[VMEM] * len(splits),
        out_specs=VMEM,
        out_shape=whole((rows, 3 * D + FF), f32),
        compiler_params=ROOM,
        cost_estimate=LIGHT,
        name="join_columns",
    )(*splits)


def product_kernel(number, owners, *refs):
    parts, (weight, hats), (*outs, sums) = refs[:number], refs[number : number + 2], refs[number + 2 :]
    rows = outs[0].shape[0]
    half = len(outs) // 2
    gain = shift = 0.0
    for low in (half, 0):
        there = [
            pl.ds(pl.multiple_of(owners[low + k] * rows, rows), rows) for k in range(half)
        ]
        total, at = None, 0
        for part in parts:
            size = part.shape[1]
            taken = jnp.concatenate([part[rows_k, :] for rows_k in there])
            term = dot(taken, weight[:, at : at + size], ((1,), (1,)))
            total = term if total is None else total + term
            at += size
        hat = jnp.concatenate([hats[rows_k, :] for rows_k in there]).astype(f32)
        gain += jnp.sum(total * hat, axis=0, keepdims=True)
        shift += jnp.sum(total, axis=0, keepdims=True)
        for k in range(half):
            out = outs[low + k]
            out[...] = total[k * rows : (k + 1) * rows].astype(out.dtype)
    sums[0:1, :] = gain
    sums[1:2, :] = shift


def product_blocks(parts, weight, hats, owners, count):
    rows = parts[0].shape[0] // count
    depth = sum(part.shape[1] for part in parts)
    tile = D // 4
    return pl.pallas_call(
        functools.partial(product_kernel, len(parts)),
        grid_spec=pltpu.PrefetchScalarGridSpec(
            num_scalar_prefetch=1,
            grid=(D // tile,),
            in_specs=[pl.BlockSpec(part.shape, lambda n, *_: (0, 0)) for part in parts]
            + [
                pl.BlockSpec((tile, depth), lambda n, *_: (n, 0)),
                pl.BlockSpec((rows * count, tile), lambda n, *_: (0, n)),
            ],
            out_specs=[pl.BlockSpec((rows, tile), lambda n, *_: (0, n))] * count
            + [pl.BlockSpec((8, tile), lambda n, *_: (0, n))],
        ),
        out_shape=[whole((rows, D), f32)] * (count // 2)
        + [whole((rows, D), bf16)] * (count // 2)
        + [whole((8, D), f32)],
        compiler_params=ROOM,
        cost_estimate=LIGHT,
        name="product_blocks",
    )(owners, *parts, weight, hats)


class Rounds:
    def __init__(self, thread):
        self.thread = thread

    def pass_through(self, *values):
        *values, self.thread = lax.optimization_barrier((*values, self.thread))
        return tuple(values)

    def begin(self, *values):
        values = self.pass_through(*values)
        return values[0] if len(values) == 1 else values

    def end(self, *values):
        return self.pass_through(*values)


def shift_pairs(size, by):
    return [(k, (k + by) % size) for k in range(size)]


def flip_pairs(size, bit):
    return [(k, k ^ bit) for k in range(size)]


def to_y(value):
    return lax.ppermute(value, "ctx", flip_pairs(lax.axis_size("ctx"), 1))


def to_z(value, by):
    return lax.ppermute(value, "ctx", shift_pairs(lax.axis_size("ctx"), 2 * by))


def to_x(value):
    return lax.ppermute(value, "dp", flip_pairs(4, 2))


def to_core(value):
    return lax.ppermute(value, "dp", flip_pairs(4, 1))


def small_steps():
    steps = []
    for axis in ("ctx", "dp"):
        bit = 1
        while bit < lax.axis_size(axis):
            steps.append((axis, bit, (lax.axis_index(axis) & bit) != 0))
            bit *= 2
    return steps


def swap(value, axis, bit):
    return lax.ppermute(value, axis, flip_pairs(lax.axis_size(axis), bit))


def halve(held, upper):
    half = held.shape[0] // 2
    low, high = held[:half], held[half:]
    return jnp.where(upper, low, high), jnp.where(upper, high, low)


def unit_rounds(count):
    edges = []
    for m in range(5 * count):
        owner, slot = (m // 4, m % 4) if m < 4 * count else (m - 4 * count, 4)
        edges.append((m // 5, m % 5, owner, slot))
    rounds = []
    left = list(edges)
    for _ in range(5):
        by_source = [[e for e in left if e[0] == s] for s in range(count)]
        taken = {}

        def place_edge(source, seen):
            for edge in by_source[source]:
                if edge[2] in seen:
                    continue
                seen.add(edge[2])
                if edge[2] not in taken or place_edge(taken[edge[2]][0], seen):
                    taken[edge[2]] = edge
                    return True
            return False

        for source in range(count):
            assert place_edge(source, set())
        chosen = {edge[0]: edge for edge in taken.values()}
        rounds.append([chosen[s] for s in range(count)])
        for edge in taken.values():
            left.remove(edge)
    return rounds


def unit_table(count, back):
    table, rounds = [[0] * 10 for _ in range(count)], []
    for turn, chosen in enumerate(unit_rounds(count)):
        pairs = []
        for source, unit, owner, slot in chosen:
            if back:
                source, unit, owner, slot = owner, slot, source, unit
            pairs.append((source, owner))
            table[source][turn] = unit
            table[owner][5 + turn] = slot
        rounds.append(pairs)
    return jnp.array(table, jnp.int32), rounds


def unit_out_kernel(units, block, *outs):
    rows = outs[0].shape[0]
    for turn, out in enumerate(outs):
        out[...] = block[pl.ds(pl.multiple_of(units[turn] * rows, rows), rows), :]


def unit_in_kernel(units, first, block, *refs):
    *gots, out = refs
    rows = gots[0].shape[0]

    @pl.when(first[0] == 1)
    def _():
        for turn, got in enumerate(gots):
            at = pl.multiple_of(units[5 + turn] * rows, rows)
            out[pl.ds(at, rows), :] = got[...].astype(out.dtype)

    @pl.when(first[0] == 0)
    def _():
        out[...] = block[...].astype(out.dtype)


class Units:
    def __init__(self, back, first):
        self.count = lax.axis_size("ctx")
        table, self.rounds = unit_table(self.count, back)
        self.units = table[lax.axis_index("ctx")]
        self.first = first.astype(jnp.int32)[None]

    def split(self, block):
        rows, columns = block.shape
        return pl.pallas_call(
            unit_out_kernel,
            in_specs=[SMEM, VMEM],
            out_specs=[VMEM] * 5,
            out_shape=[whole((rows // 5, columns), bf16)] * 5,
            compiler_params=ROOM,
            cost_estimate=LIGHT,
            name="unit_out",
        )(self.units, block)

    def send(self, parts, turn):
        return lax.ppermute(parts[turn], ("dp", "ctx"), self.rounds[turn])

    def merge(self, block, got, dtype):
        return pl.pallas_call(
            unit_in_kernel,
            in_specs=[SMEM, SMEM] + [VMEM] * 6,
            out_specs=VMEM,
            out_shape=whole(block.shape, dtype),
            compiler_params=ROOM,
            cost_estimate=LIGHT,
            name="unit_in",
        )(self.units, self.first, block, *got)


def local(
    tokens, norm_gain, norm_shift, input_weight, input_bias, output_weight, output_bias, cotangent
):
    count = lax.axis_size("ctx")
    place = lax.axis_index("ctx")
    dp_place = lax.axis_index("dp")
    far = count // 2
    z, y = place // 2, place % 2
    devices = 4 * count
    own = D // count
    length = 2 * BLK * count
    rows_out = output_weight.shape[0]
    token_block = tokens.reshape(2 * BLK, D)
    grad_block = cotangent.reshape(2 * BLK, D)

    stored = [min(b, 2 * count - 1 - b) * 2 * BLK + BLK * (b >= count) for b in range(2 * count)]
    steps = jnp.arange(far, dtype=jnp.int32)
    owners_mine = ((z + far - steps) % far) * 2 + y
    owners = jnp.concatenate([owners_mine, owners_mine ^ 1])
    rounds = Rounds(grad_block)
    gather = lambda v, axis: lax.all_gather(v, axis, axis=0, tiled=True)
    scatter = lambda v, axis: lax.psum_scatter(v, axis, scatter_dimension=0, tiled=True)

    small = jnp.concatenate([norm_gain, norm_shift, input_bias, output_bias])
    cuts = [norm_gain.shape[0], norm_shift.shape[0], input_bias.shape[0], output_bias.shape[0]]
    ends = [sum(cuts[: k + 1]) for k in range(4)]
    units = Units(False, dp_place == 0)
    packed = split_columns(input_weight, count)
    held, other = [token_block, to_z(token_block, 1)], [to_y(token_block)]
    grad_held, grad_other = [grad_block], [to_y(grad_block)]
    columns = lax.all_to_all(packed, "ctx", 0, 0, tiled=True)
    unit_parts = units.split(output_weight)
    unit_got = []
    tables = rotary_tables(length, min(128, own))
    vectors = small[None]
    for axis, bit, upper in small_steps():
        got = swap(vectors, axis, bit)
        vectors = jnp.where(
            upper, jnp.concatenate([got, vectors]), jnp.concatenate([vectors, got])
        )
    tables = tuple(tables)
    first = rounds.end(held[1], other[0], grad_other[0], columns, vectors, *tables, *unit_parts)
    held[1], other[0], grad_other[0], columns, vectors, *tables = first[:7]
    unit_parts = first[7:]
    weight_in = gather(columns.reshape(-1, columns.shape[-1]), "dp")
    gain, shift, bias_in, bias_out = (
        vectors[:, end - cut : end].reshape(-1).astype(f32) for cut, end in zip(cuts, ends)
    )
    bias_own = jnp.concatenate(
        [lax.dynamic_slice_in_dim(bias_in, start, width) for start, width in column_pieces(place, count)]
    )

    gelu = lambda v: jax.nn.gelu(v, approximate=True)
    for step in range(1, far):
        last = step == far - 1
        source = rounds.begin(held[step])
        turns = range(len(unit_got), 5 if last else min(5, len(unit_got) + 2))
        got, ahead, *moved = rounds.end(
            to_y(source),
            to_z(rounds.begin(grad_block) if last else source, 1),
            *[units.send(rounds.begin(*unit_parts), turn) for turn in turns],
        )
        unit_got += moved
        other.append(got)
        (grad_held if last else held).append(ahead)

    weight_out = gather(units.merge(output_weight, unit_got, bf16), "dp")

    kept = {}

    def first_products(step):
        if step == 1:
            normed, hats = norm_blocks(rounds.begin(*held, *other), owners, gain, shift)
            qkv = dot(normed, weight_in[:, : 3 * own], ((1,), (0,))) + bias_own[: 3 * own]
            return dict(normed=normed, hats=hats, qkv=qkv)
        if step == 2:
            names = ("attended", "queries", "keys", "values", "stats")
            return dict(zip(names, attention_forward(rounds.begin(kept["qkv"]), own, stored, tables)))
        if step == 3:
            hidden = dot(rounds.begin(kept["normed"]), weight_in[:, 3 * own :], ((1,), (0,)))
            hidden += bias_own[3 * own :]
            activated, slope = jax.jvp(gelu, (hidden,), (jnp.ones_like(hidden),))
            return dict(slope=slope, activated=activated.astype(bf16))
        return {}

    for step in range(1, far):
        source = rounds.begin(grad_held[step])
        started = [to_y(source)]
        if step < far - 1:
            started.append(to_z(source, 1))
        sends = len(started)
        made = first_products(step)
        started = rounds.end(*started, *made.values())
        kept.update(zip(made, started[sends:]))
        grad_other.append(started[0])
        grad_held += started[1:sends]
    normed, hats = kept["normed"], kept["hats"]
    branch = jnp.concatenate(rounds.begin(kept["attended"], kept["activated"]), axis=1)
    out_part = dot(branch, weight_out, ((1,), (0,))).astype(bf16)
    out_part = rounds.end(out_part)[0]
    out_sum = scatter(out_part, "ctx")
    grads = order_blocks(rounds.begin(*grad_held, *grad_other), owners)

    part = D // 4
    near = lambda r: lax.dynamic_slice_in_dim(normed, (dp_place ^ r) * part, part, 1)
    term = lambda r, chunk: dot(near(r), chunk, ((0,), (0,)))
    far_terms = lambda chunk: jnp.concatenate([term(1, chunk), term(3, chunk)]).astype(bf16)
    mid_terms = lambda chunk, got: (term(2, chunk) + got[part:].astype(f32)).astype(bf16)

    def near_terms(chunk, got, across):
        total = term(0, chunk) + got[:part].astype(f32) + across.astype(f32)
        return total.astype(bf16).reshape(count, part // count, -1)

    spread = lambda v: lax.all_to_all(v, "ctx", 0, 0, tiled=True)
    grad_up = (kept["slope"] * dot(grads, weight_out[own:], ((1,), (1,)))).astype(bf16)
    beside = to_core(far_terms(grad_up))
    grad_mix = dot(grads, weight_out[:own], ((1,), (1,))).astype(bf16)
    beside, grad_mix = rounds.end(beside, grad_mix)
    middle = mid_terms(grad_up, beside)
    middle, *saved = rounds.begin(middle, *[kept[name] for name in ("queries", "keys", "values", "stats")])
    across = to_x(middle)
    grad_qkv = attention_backward(
        saved,
        grad_mix,
        stored,
        tables,
    )
    grad_heads = jnp.concatenate(grad_qkv, axis=1)
    sent_heads = far_terms(grad_heads)
    across, sent_heads, *grad_qkv = rounds.end(across, sent_heads, *grad_qkv)

    sent_mlp, sent_heads, *grad_qkv = rounds.begin(near_terms(grad_up, beside, across), sent_heads, *grad_qkv)
    came_mlp = spread(sent_mlp)
    beside_heads = to_core(sent_heads)
    *normed_terms, sums = product_blocks([*grad_qkv, grad_up], weight_in, hats, owners, count)
    branch, sums = rounds.begin(branch, sums)
    out_term = dot(branch, grads, ((0,), (0,))).astype(bf16)
    came_mlp, beside, out_term, sums, *normed_terms = rounds.end(
        came_mlp, beside_heads, out_term, sums, *normed_terms
    )
    out_near = lambda r: lax.dynamic_slice_in_dim(out_term, (dp_place ^ r) * rows_out, rows_out, 0)

    bias_terms = [jnp.sum(v.astype(f32), axis=0) for v in grad_qkv]
    up_terms, at = jnp.sum(grad_up.astype(f32), axis=0), 0
    for _, width in column_pieces(0, count)[3:]:
        bias_terms.append(up_terms[at : at + width])
        at += width
    here = (jnp.arange(count) == place).astype(f32)[:, None]
    vector_terms = jnp.concatenate(
        [
            sums[0].reshape(devices, -1),
            sums[1].reshape(devices, -1),
            jnp.concatenate([(here * t[None]).reshape(-1) for t in bias_terms]).reshape(devices, -1),
            jnp.sum(grad_block.astype(f32), axis=0).reshape(devices, -1),
        ],
        axis=1,
    )
    small_left = small_steps()[::-1]

    def small_step(terms):
        axis, bit, upper = small_left.pop(0)
        give, keep = halve(terms, upper)
        return swap(give, axis, bit), keep

    mine, theirs = normed_terms[:far], normed_terms[far:]
    got, running = [None] * far, None
    back = Units(True, dp_place == 0)
    back_parts, back_got = None, []
    left_y, left_z, stage = list(range(far))[::-1], list(range(1, far))[::-1], 0
    across = came_heads = None
    while left_y or left_z or stage < 4:
        names, started = [], []

        def start(name, value):
            names.append(name)
            started.append(value)

        z_now = left_z[0] if left_z and got[left_z[0]] is not None else None
        pair = left_y[:2]
        left_y = left_y[2:]
        for k in pair:
            start(("y", k), to_y(rounds.begin(theirs[k])))
        if z_now is not None:
            left_z.pop(0)
            joint = mine[z_now] + got[z_now].astype(f32)
            if running is not None:
                joint = joint + running.astype(f32)
            start("z", to_z(rounds.begin(joint.astype(bf16)), -1))
        if stage == 0:
            start("x", to_x(rounds.begin(mid_terms(grad_heads, beside))))
            start("core", to_core(rounds.begin(jnp.concatenate([out_near(1), out_near(3)]))))
        elif stage == 1:
            block_out = (token_block.astype(f32) + rounds.begin(out_sum).astype(f32) + bias_out).astype(bf16)
            start("block", block_out)
            start("spread", spread(rounds.begin(near_terms(grad_heads, beside, across))))
            middle = out_near(2).astype(f32) + out_beside[rows_out:].astype(f32)
            start("x", to_x(rounds.begin(middle.astype(bf16))))
        if stage >= 2 and len(back_got) < 5:
            if back_parts is None:
                out_own = out_near(0).astype(f32) + out_beside[:rows_out].astype(f32)
                out_own = (out_own + across.astype(f32)).astype(bf16)
                back_parts = back.split(rounds.begin(out_own))
            for turn in range(len(back_got), min(5, len(back_got) + 3)):
                start("unit", back.send(back_parts, turn))
        if small_left:
            give, keep = small_step(rounds.begin(vector_terms))
            start("give", give)
            start("keep", keep)
        stage += 1
        for name, value in zip(names, rounds.end(*started)):
            if name == "z":
                running = value
            elif name == "core":
                out_beside = value
            elif name == "block":
                block_out = value
            elif name == "x":
                across = value
            elif name == "spread":
                came_heads = value
            elif name == "unit":
                back_got.append(value)
            elif name == "give":
                vector_terms = value
            elif name == "keep":
                vector_terms = vector_terms + value
            else:
                got[name[1]] = value
    joined = lambda step: mine[step] + got[step].astype(f32)
    weightin_grad = join_columns([came_heads, came_mlp], [slice(0, 3), slice(3, None)], count)
    weightout_grad = back.merge(out_own, back_got, f32)
    while small_left:
        give, keep = small_step(vector_terms)
        vector_terms = give + keep
    gain_grad, shift_grad, biasin_grad, biasout_grad = (
        vector_terms[0, end - cut : end] for cut, end in zip(cuts, ends)
    )

    own_normed = joined(0) + running.astype(f32)
    own_x = token_block.astype(f32)
    centred = own_x - jnp.mean(own_x, axis=-1, keepdims=True)
    scale = lax.rsqrt(jnp.mean(centred * centred, axis=-1, keepdims=True) + epsilon)
    hat = centred * scale
    g = own_normed * gain
    tokens_grad = rounds.thread.astype(f32) + scale * (
        g - jnp.mean(g, axis=-1, keepdims=True) - hat * jnp.mean(g * hat, axis=-1, keepdims=True)
    )
    return (
        block_out.reshape(tokens.shape),
        tokens_grad.reshape(tokens.shape),
        gain_grad,
        shift_grad,
        weightin_grad,
        biasin_grad,
        weightout_grad,
        biasout_grad,
    )


def solution(mesh):
    placed = (
        P("dp", None, "ctx", None, None),
        P(("dp", "ctx")),
        P(("dp", "ctx")),
        P(("dp", "ctx"), None),
        P(("dp", "ctx")),
        P(("dp", "ctx"), None),
        P(("dp", "ctx")),
        P("dp", None, "ctx", None, None),
    )
    return jax.shard_map(
        local,
        mesh=mesh,
        in_specs=placed,
        out_specs=(
            P("dp", None, "ctx", None, None),
            P("dp", None, "ctx", None, None),
            P(("dp", "ctx")),
            P(("dp", "ctx")),
            P(("dp", "ctx"), None),
            P(("dp", "ctx")),
            P(("dp", "ctx"), None),
            P(("dp", "ctx")),
        ),
        check_vma=False,
    )
```

```python
import functools
import math

import jax
import jax.numpy as jnp
from jax import lax
from jax.experimental import pallas as pl
from jax.experimental.pallas import tpu as pltpu
from jax.sharding import PartitionSpec as P

D = 2048
HEADS = 32
HEAD = 64
ROT = 32
BLK = 64
FF = 8192
TILE = 256

epsilon = 1e-05
theta_log = math.log(10000.0)
masked_fill = -1e30
bf16 = jnp.bfloat16
f32 = jnp.float32


def dot(a, b, dims):
    return lax.dot_general(a, b, (dims, ((), ())), preferred_element_type=f32)


def whole(shape, dtype):
    return jax.ShapeDtypeStruct(shape, dtype)


VMEM = pl.BlockSpec(memory_space=pltpu.VMEM)
SMEM = pl.BlockSpec(memory_space=pltpu.SMEM)
ROOM = pltpu.CompilerParams(vmem_limit_bytes=56 * 2**20)
LIGHT = pl.CostEstimate(flops=1, bytes_accessed=1, transcendentals=0)


def turn_lanes(values, cos, sin, sign):
    half = ROT // 2
    width = values.shape[-1]
    place = lax.broadcasted_iota(jnp.int32, (1, width), 1) % HEAD
    ahead = pltpu.roll(values, width - half, 1)
    behind = pltpu.roll(values, half, 1)
    turned = values * cos + sign * sin * jnp.where(place < half, -ahead, behind)
    return jnp.where(place < ROT, turned, values)


def head_scores(keys, q_head, start, reach, tile):
    scores = dot(keys, q_head * 0.125, ((1,), (1,)))
    if isinstance(start, int):
        before, start, reach = scores[:start], 0, reach - start
        scores = scores[-reach:]
    else:
        before = scores[:0]
    allowed = lax.broadcasted_iota(jnp.int32, (reach, tile), 0) <= start + (
        lax.broadcasted_iota(jnp.int32, (reach, tile), 1)
    )
    scores = jnp.where(allowed, scores, masked_fill)
    return jnp.concatenate([before, scores]) if before.shape[0] else scores


def for_row_tiles(length, tile, body):
    count = length // tile
    if count <= 4:
        for step in range(count):
            body(step * tile, (step + 1) * tile)
    else:
        per = count // 4
        for part in range(4):

            @pl.loop(part * per, (part + 1) * per)
            def _(step, part=part):
                body(pl.multiple_of(step * tile, tile), (part + 1) * per * tile)


def forward_kernel(length, width, stored, hq, hk, hv, cos, sin, att, qs, ks, vs, stats, raw, vt):
    lanes = lax.broadcasted_iota(jnp.int32, (1, width), 1)
    tile = min(TILE, length)
    blocks = length // BLK
    cos_all, sin_all = cos[...], sin[...]

    def natural(ref):
        for b in range(blocks):
            raw[b * BLK : (b + 1) * BLK, :] = ref[stored[b] : stored[b] + BLK, :]
        return raw[...]

    qs[...] = turn_lanes(natural(hq), cos_all, sin_all, 1.0).astype(bf16)
    ks[...] = turn_lanes(natural(hk), cos_all, sin_all, 1.0).astype(bf16)
    values = natural(hv)
    vs[...] = values.astype(bf16)
    vt[...] = values.T.astype(bf16)

    def body(start, reach):
        rows = pl.ds(start, tile)
        q_rows = qs[rows, :]
        keys = ks[0:reach, :]
        mixes = []
        for head in range(width // HEAD):
            mine = (lanes // HEAD) == head
            q_head = jnp.where(mine, q_rows, jnp.zeros_like(q_rows))
            scores = head_scores(keys, q_head, start, reach, tile)
            top = jnp.max(scores, axis=0, keepdims=True)
            weights = jnp.exp(scores - top)
            part = 1.0 / jnp.sum(weights, axis=0, keepdims=True)
            stats[0, 2 * head : 2 * head + 1, rows] = top
            stats[0, 2 * head + 1 : 2 * head + 2, rows] = part
            low = (weights * part).astype(bf16)
            mixes.append(dot(vt[head * HEAD : (head + 1) * HEAD, 0:reach], low, ((1,), (0,))))
        raw[rows, :] = jnp.concatenate(mixes, axis=0).T

    for_row_tiles(length, tile, body)
    for b in range(blocks):
        att[stored[b] : stored[b] + BLK, :] = raw[b * BLK : (b + 1) * BLK, :].astype(bf16)


def backward_kernel(length, width, stored, qs, ks, vs, stats, gm, cos, sin, gq, gk, gv, gs, kt, dq, dk, dv):
    lanes = lax.broadcasted_iota(jnp.int32, (1, width), 1)
    tile = min(TILE, length)
    blocks = length // BLK
    for b in range(blocks):
        gs[b * BLK : (b + 1) * BLK, :] = gm[stored[b] : stored[b] + BLK, :]
    kt[...] = ks[...].T
    dk[...] = jnp.zeros_like(dk)
    dv[...] = jnp.zeros_like(dv)

    def body(start, reach):
        rows = pl.ds(start, tile)
        q_rows = qs[rows, :]
        g_rows = gs[rows, :]
        keys = ks[0:reach, :]
        vals = vs[0:reach, :]
        gqs = []
        for head in range(width // HEAD):
            mine = (lanes // HEAD) == head
            q_head = jnp.where(mine, q_rows, jnp.zeros_like(q_rows))
            g_head = jnp.where(mine, g_rows, jnp.zeros_like(g_rows))
            scores = head_scores(keys, q_head, start, reach, tile)
            top = stats[0, 2 * head : 2 * head + 1, rows]
            part = stats[0, 2 * head + 1 : 2 * head + 2, rows]
            shares = jnp.exp(scores - top) * part
            grad_shares = dot(vals, g_head, ((1,), (1,)))
            moved = shares * grad_shares
            inner = jnp.sum(moved, axis=0, keepdims=True)
            grad_scores = (moved - shares * inner).astype(bf16)
            gqs.append(dot(kt[head * HEAD : (head + 1) * HEAD, 0:reach], grad_scores, ((1,), (0,))))
            dv[0:reach, :] += dot(shares.astype(bf16), g_head, ((1,), (0,)))
            dk[0:reach, :] += dot(grad_scores, q_head, ((1,), (0,)))
        grad_q = jnp.concatenate(gqs, axis=0).T * 0.125
        dq[rows, :] = turn_lanes(grad_q, cos[rows, :], sin[rows, :], -1.0).astype(bf16)

    for_row_tiles(length, tile, body)
    grad_k = turn_lanes(dk[...] * 0.125, cos[...], sin[...], -1.0).astype(bf16)
    grad_v = dv[...].astype(bf16)
    for b in range(blocks):
        here, there = slice(b * BLK, (b + 1) * BLK), slice(stored[b], stored[b] + BLK)
        gq[there, :] = dq[here, :]
        gk[there, :] = grad_k[here]
        gv[there, :] = grad_v[here]


def rotary_tables(length, width):
    frequency = jnp.exp(-theta_log * 2.0 * jnp.arange(ROT // 2).astype(f32) / ROT)
    angles = jnp.arange(length, dtype=jnp.int32).astype(f32)[:, None] * frequency[None, :]
    spare = jnp.zeros((length, HEAD - ROT), f32)
    repeat = width // HEAD
    cos = jnp.tile(jnp.concatenate([jnp.cos(angles)] * 2 + [spare], axis=1), (1, repeat))
    sin = jnp.tile(jnp.concatenate([jnp.sin(angles)] * 2 + [spare], axis=1), (1, repeat))
    return cos, sin


def attention_specs(length, columns):
    width = min(128, columns)
    groups = columns // width
    group = pl.BlockSpec((length, width), lambda g: (0, g))
    table = pl.BlockSpec((length, width), lambda g: (0, 0))
    stats = pl.BlockSpec((1, 8, length), lambda g: (g, 0, 0))
    return width, groups, group, table, stats


def attention_forward(hidden, columns, stored, tables):
    length = hidden.shape[0]
    width, groups, group, table, stats = attention_specs(length, columns)
    if width < 128:
        parts = [hidden[:, k * columns : (k + 1) * columns] for k in range(3)]
        specs = [group] * 3
    else:
        parts = [hidden] * 3
        specs = [pl.BlockSpec((length, width), lambda g, k=k: (0, k * groups + g)) for k in range(3)]
    return pl.pallas_call(
        functools.partial(forward_kernel, length, width, stored),
        grid=(groups,),
        in_specs=specs + [table, table],
        out_specs=[group] * 4 + [stats],
        out_shape=[whole((length, columns), bf16)] * 4 + [whole((groups, 8, length), f32)],
        scratch_shapes=[pltpu.VMEM((length, width), f32), pltpu.VMEM((width, length), bf16)],
        compiler_params=ROOM,
        cost_estimate=LIGHT,
        name="attention_forward",
    )(*parts, *tables)


def attention_backward(kept, grad_mix, stored, tables):
    length, columns = grad_mix.shape
    width, groups, group, table, stats = attention_specs(length, columns)
    return pl.pallas_call(
        functools.partial(backward_kernel, length, width, stored),
        grid=(groups,),
        in_specs=[group] * 3 + [stats, group, table, table],
        out_specs=[group] * 3,
        out_shape=[whole((length, columns), bf16)] * 3,
        scratch_shapes=[
            pltpu.VMEM((length, width), bf16),
            pltpu.VMEM((width, length), bf16),
            pltpu.VMEM((length, width), bf16),
            pltpu.VMEM((length, width), f32),
            pltpu.VMEM((length, width), f32),
        ],
        compiler_params=ROOM,
        cost_estimate=LIGHT,
        name="attention_backward",
    )(*kept, grad_mix, *tables)


def norm_kernel(owners, gain, shift, *refs):
    blocks, (normed, hats) = refs[:-2], refs[-2:]
    rows = blocks[0].shape[0]
    for b, ref in enumerate(blocks):
        x = ref[...].astype(f32)
        centred = x - jnp.mean(x, axis=-1, keepdims=True)
        hat = centred * lax.rsqrt(jnp.mean(centred * centred, axis=-1, keepdims=True) + epsilon)
        there = pl.ds(pl.multiple_of(owners[b] * rows, rows), rows)
        normed[there, :] = (hat * gain[...] + shift[...]).astype(bf16)
        hats[there, :] = hat.astype(bf16)


def norm_blocks(blocks, owners, gain, shift):
    rows = blocks[0].shape[0]
    total = rows * len(blocks)
    if total > 1024:
        normed = hats = jnp.zeros((total, D), bf16)
        for b, block in enumerate(blocks):
            x = block.astype(f32)
            centred = x - jnp.mean(x, axis=-1, keepdims=True)
            spread = jnp.mean(centred * centred, axis=-1, keepdims=True)
            hat = centred * lax.rsqrt(spread + epsilon)
            at = (owners[b] * rows, 0)
            normed = lax.dynamic_update_slice(normed, (hat * gain + shift).astype(bf16), at)
            hats = lax.dynamic_update_slice(hats, hat.astype(bf16), at)
        return normed, hats
    return pl.pallas_call(
        norm_kernel,
        in_specs=[SMEM] + [VMEM] * (2 + len(blocks)),
        out_specs=[VMEM] * 2,
        out_shape=[whole((total, D), bf16)] * 2,
        compiler_params=ROOM,
        cost_estimate=LIGHT,
        name="norm",
    )(owners, gain[None], shift[None], *blocks)


def order_kernel(owners, *refs):
    *blocks, out = refs
    rows = blocks[0].shape[0]
    for b, ref in enumerate(blocks):
        out[pl.ds(pl.multiple_of(owners[b] * rows, rows), rows), :] = ref[...]


def order_blocks(blocks, owners):
    rows, columns = blocks[0].shape
    return pl.pallas_call(
        order_kernel,
        in_specs=[SMEM] + [VMEM] * len(blocks),
        out_specs=VMEM,
        out_shape=whole((rows * len(blocks), columns), blocks[0].dtype),
        compiler_params=ROOM,
        cost_estimate=LIGHT,
        name="order_blocks",
    )(owners, *blocks)


def hidden_kernel(heads, normed, weight, bias, qkv, activated, slope):
    step = pl.program_id(0)
    rows = normed.shape[0]
    blocks = [slice(at, at + rows) for at in range(0, normed.shape[0], rows)]

    @pl.when(step < heads)
    def _():
        for span in blocks:
            qkv[span, :] = dot(normed[span, :], weight[...], ((1,), (0,))) + bias[...]

    @pl.when(step >= heads)
    def _():
        for span in blocks:
            v = dot(normed[span, :], weight[...], ((1,), (0,))) + bias[...]
            squared = v * v
            bend = jnp.tanh(0.7978845608 * v * (1.0 + 0.044715 * squared))
            half = 0.5 * (1.0 + bend)
            activated[span, :] = (v * half).astype(bf16)
            inner = 0.7978845608 * (1.0 + 3 * 0.044715 * squared)
            slope[span, :] = half + 0.5 * v * (1.0 - bend * bend) * inner


def hidden_units(normed, weight, bias, own):
    length, tile = normed.shape[0], 256
    heads = 3 * own // tile
    rest = weight.shape[1] - 3 * own
    if 3 * own % tile or rest % tile or length > 1024:
        gelu = lambda v: jax.nn.gelu(v, approximate=True)
        hidden = dot(normed, weight, ((1,), (0,))) + bias
        activated, slope = jax.jvp(
            gelu, (hidden[:, 3 * own :],), (jnp.ones((length, rest), f32),)
        )
        return hidden[:, : 3 * own], activated.astype(bf16), slope
    late = pl.BlockSpec((length, tile), lambda n: (0, jnp.maximum(n - heads, 0)))
    return pl.pallas_call(
        functools.partial(hidden_kernel, heads),
        grid=(weight.shape[1] // tile,),
        in_specs=[
            pl.BlockSpec((length, D), lambda n: (0, 0)),
            pl.BlockSpec((D, tile), lambda n: (0, n)),
            pl.BlockSpec((1, tile), lambda n: (0, n)),
        ],
        out_specs=[
            pl.BlockSpec((length, tile), lambda n: (0, jnp.minimum(n, heads - 1))),
            late,
            late,
        ],
        out_shape=[whole((length, 3 * own), f32), whole((length, rest), bf16), whole((length, rest), f32)],
        compiler_params=ROOM,
        cost_estimate=LIGHT,
        name="hidden_units",
    )(normed, weight, bias[None])


def column_pieces(index, count):
    own = D // count
    rows = (D + FF) // (4 * count)
    pieces = [(which * D + index * own, own) for which in range(3)]
    pieces.append((3 * D + index * (rows - own), rows - own))
    for part in range(1, 4):
        pieces.append((3 * D + part * rows * count - D + index * rows, rows))
    return pieces


def split_kernel(count, weight, out):
    for index in range(count):
        at = 0
        for start, width in column_pieces(index, count):
            out[index, :, at : at + width] = weight[:, start : start + width]
            at += width


def split_columns(weight, count):
    rows, columns = weight.shape
    return pl.pallas_call(
        functools.partial(split_kernel, count),
        in_specs=[VMEM],
        out_specs=VMEM,
        out_shape=whole((count, rows, columns // count), weight.dtype),
        compiler_params=ROOM,
        cost_estimate=LIGHT,
        name="split_columns",
    )(weight)


def join_kernel(count, spans, *refs):
    *splits, out = refs
    for split, span in zip(splits, spans):
        for index in range(count):
            at = 0
            for start, width in column_pieces(index, count)[span]:
                out[:, start : start + width] = split[index, :, at : at + width].astype(f32)
                at += width


def join_columns(splits, spans, count):
    rows = splits[0].shape[1]
    return pl.pallas_call(
        functools.partial(join_kernel, count, spans),
        in_specs=[VMEM] * len(splits),
        out_specs=VMEM,
        out_shape=whole((rows, 3 * D + FF), f32),
        compiler_params=ROOM,
        cost_estimate=LIGHT,
        name="join_columns",
    )(*splits)


def product_kernel(number, owners, *refs):
    parts, (weight, hats), (*outs, sums) = refs[:number], refs[number : number + 2], refs[number + 2 :]
    rows = outs[0].shape[0]
    half = len(outs) // 2
    gain = shift = 0.0
    for low in (half, 0):
        there = [
            pl.ds(pl.multiple_of(owners[low + k] * rows, rows), rows) for k in range(half)
        ]
        total, at = None, 0
        for part in parts:
            size = part.shape[1]
            taken = jnp.concatenate([part[rows_k, :] for rows_k in there])
            term = dot(taken, weight[:, at : at + size], ((1,), (1,)))
            total = term if total is None else total + term
            at += size
        hat = jnp.concatenate([hats[rows_k, :] for rows_k in there]).astype(f32)
        gain += jnp.sum(total * hat, axis=0, keepdims=True)
        shift += jnp.sum(total, axis=0, keepdims=True)
        for k in range(half):
            out = outs[low + k]
            out[...] = total[k * rows : (k + 1) * rows].astype(out.dtype)
    sums[0:1, :] = gain
    sums[1:2, :] = shift


def product_blocks(parts, weight, hats, owners, count):
    rows = parts[0].shape[0] // count
    depth = sum(part.shape[1] for part in parts)
    tile = D // 4
    return pl.pallas_call(
        functools.partial(product_kernel, len(parts)),
        grid_spec=pltpu.PrefetchScalarGridSpec(
            num_scalar_prefetch=1,
            grid=(D // tile,),
            in_specs=[pl.BlockSpec(part.shape, lambda n, *_: (0, 0)) for part in parts]
            + [
                pl.BlockSpec((tile, depth), lambda n, *_: (n, 0)),
                pl.BlockSpec((rows * count, tile), lambda n, *_: (0, n)),
            ],
            out_specs=[pl.BlockSpec((rows, tile), lambda n, *_: (0, n))] * count
            + [pl.BlockSpec((8, tile), lambda n, *_: (0, n))],
        ),
        out_shape=[whole((rows, D), f32)] * (count // 2)
        + [whole((rows, D), bf16)] * (count // 2)
        + [whole((8, D), f32)],
        compiler_params=ROOM,
        cost_estimate=LIGHT,
        name="product_blocks",
    )(owners, *parts, weight, hats)


class Rounds:
    def __init__(self, thread):
        self.thread = thread

    def pass_through(self, *values):
        *values, self.thread = lax.optimization_barrier((*values, self.thread))
        return tuple(values)

    def begin(self, *values):
        values = self.pass_through(*values)
        return values[0] if len(values) == 1 else values

    def end(self, *values):
        return self.pass_through(*values)


def shift_pairs(size, by):
    return [(k, (k + by) % size) for k in range(size)]


def flip_pairs(size, bit):
    return [(k, k ^ bit) for k in range(size)]


def to_y(value):
    return lax.ppermute(value, "ctx", flip_pairs(lax.axis_size("ctx"), 1))


def to_z(value, by):
    return lax.ppermute(value, "ctx", shift_pairs(lax.axis_size("ctx"), 2 * by))


def to_x(value):
    return lax.ppermute(value, "dp", flip_pairs(4, 2))


def to_core(value):
    return lax.ppermute(value, "dp", flip_pairs(4, 1))


def small_steps():
    steps = []
    for axis in ("ctx", "dp"):
        bit = 1
        while bit < lax.axis_size(axis):
            steps.append((axis, bit, (lax.axis_index(axis) & bit) != 0))
            bit *= 2
    return steps


def swap(value, axis, bit):
    return lax.ppermute(value, axis, flip_pairs(lax.axis_size(axis), bit))


def halve(held, upper):
    half = held.shape[0] // 2
    low, high = held[:half], held[half:]
    return jnp.where(upper, low, high), jnp.where(upper, high, low)


def unit_rounds(count):
    edges = []
    for m in range(5 * count):
        owner, slot = (m // 4, m % 4) if m < 4 * count else (m - 4 * count, 4)
        edges.append((m // 5, m % 5, owner, slot))
    rounds = []
    left = list(edges)
    for _ in range(5):
        by_source = [[e for e in left if e[0] == s] for s in range(count)]
        taken = {}

        def place_edge(source, seen):
            for edge in by_source[source]:
                if edge[2] in seen:
                    continue
                seen.add(edge[2])
                if edge[2] not in taken or place_edge(taken[edge[2]][0], seen):
                    taken[edge[2]] = edge
                    return True
            return False

        for source in range(count):
            assert place_edge(source, set())
        chosen = {edge[0]: edge for edge in taken.values()}
        rounds.append([chosen[s] for s in range(count)])
        for edge in taken.values():
            left.remove(edge)
    return rounds


def unit_table(count, back):
    table, rounds = [[0] * 10 for _ in range(count)], []
    for turn, chosen in enumerate(unit_rounds(count)):
        pairs = []
        for source, unit, owner, slot in chosen:
            if back:
                source, unit, owner, slot = owner, slot, source, unit
            pairs.append((source, owner))
            table[source][turn] = unit
            table[owner][5 + turn] = slot
        rounds.append(pairs)
    return jnp.array(table, jnp.int32), rounds


def unit_out_kernel(units, block, *outs):
    rows = outs[0].shape[0]
    for turn, out in enumerate(outs):
        out[...] = block[pl.ds(pl.multiple_of(units[turn] * rows, rows), rows), :]


def unit_in_kernel(units, first, block, *refs):
    *gots, out = refs
    rows = gots[0].shape[0]

    @pl.when(first[0] == 1)
    def _():
        for turn, got in enumerate(gots):
            at = pl.multiple_of(units[5 + turn] * rows, rows)
            out[pl.ds(at, rows), :] = got[...].astype(out.dtype)

    @pl.when(first[0] == 0)
    def _():
        out[...] = block[...].astype(out.dtype)


class Units:
    def __init__(self, back, first):
        self.count = lax.axis_size("ctx")
        table, self.rounds = unit_table(self.count, back)
        self.units = table[lax.axis_index("ctx")]
        self.first = first.astype(jnp.int32)[None]

    def split(self, block):
        rows, columns = block.shape
        return pl.pallas_call(
            unit_out_kernel,
            in_specs=[SMEM, VMEM],
            out_specs=[VMEM] * 5,
            out_shape=[whole((rows // 5, columns), bf16)] * 5,
            compiler_params=ROOM,
            cost_estimate=LIGHT,
            name="unit_out",
        )(self.units, block)

    def send(self, parts, turn):
        return lax.ppermute(parts[turn], ("dp", "ctx"), self.rounds[turn])

    def merge(self, block, got, dtype):
        return pl.pallas_call(
            unit_in_kernel,
            in_specs=[SMEM, SMEM] + [VMEM] * 6,
            out_specs=VMEM,
            out_shape=whole(block.shape, dtype),
            compiler_params=ROOM,
            cost_estimate=LIGHT,
            name="unit_in",
        )(self.units, self.first, block, *got)


def local(
    tokens, norm_gain, norm_shift, input_weight, input_bias, output_weight, output_bias, cotangent
):
    count = lax.axis_size("ctx")
    place = lax.axis_index("ctx")
    dp_place = lax.axis_index("dp")
    far = count // 2
    z, y = place // 2, place % 2
    devices = 4 * count
    own = D // count
    length = 2 * BLK * count
    rows_out = output_weight.shape[0]
    token_block = tokens.reshape(2 * BLK, D)
    grad_block = cotangent.reshape(2 * BLK, D)

    stored = [min(b, 2 * count - 1 - b) * 2 * BLK + BLK * (b >= count) for b in range(2 * count)]
    steps = jnp.arange(far, dtype=jnp.int32)
    owners_mine = ((z + far - steps) % far) * 2 + y
    owners = jnp.concatenate([owners_mine, owners_mine ^ 1])
    rounds = Rounds(grad_block)
    gather = lambda v, axis: lax.all_gather(v, axis, axis=0, tiled=True)
    scatter = lambda v, axis: lax.psum_scatter(v, axis, scatter_dimension=0, tiled=True)

    small = jnp.concatenate([norm_gain, norm_shift, input_bias, output_bias])
    cuts = [norm_gain.shape[0], norm_shift.shape[0], input_bias.shape[0], output_bias.shape[0]]
    ends = [sum(cuts[: k + 1]) for k in range(4)]
    units = Units(False, dp_place == 0)
    packed = split_columns(input_weight, count)
    held, other = [token_block, to_z(token_block, 1)], [to_y(token_block)]
    grad_held, grad_other = [grad_block], [to_y(grad_block)]
    columns = lax.all_to_all(packed, "ctx", 0, 0, tiled=True)
    unit_parts = units.split(output_weight)
    unit_got = []
    tables = rotary_tables(length, min(128, own))
    vectors = small[None]
    for axis, bit, upper in small_steps():
        got = swap(vectors, axis, bit)
        vectors = jnp.where(
            upper, jnp.concatenate([got, vectors]), jnp.concatenate([vectors, got])
        )
    tables = tuple(tables)
    first = rounds.end(held[1], other[0], grad_other[0], columns, vectors, *tables, *unit_parts)
    held[1], other[0], grad_other[0], columns, vectors, *tables = first[:7]
    unit_parts = first[7:]
    weight_in = gather(columns.reshape(-1, columns.shape[-1]), "dp")
    gain, shift, bias_in, bias_out = (
        vectors[:, end - cut : end].reshape(-1).astype(f32) for cut, end in zip(cuts, ends)
    )
    bias_own = jnp.concatenate(
        [lax.dynamic_slice_in_dim(bias_in, start, width) for start, width in column_pieces(place, count)]
    )

    for step in range(1, far):
        last = step == far - 1
        source = rounds.begin(held[step])
        turns = range(len(unit_got), 5 if last else min(5, len(unit_got) + 2))
        got, ahead, *moved = rounds.end(
            to_y(source),
            to_z(rounds.begin(grad_block) if last else source, 1),
            *[units.send(rounds.begin(*unit_parts), turn) for turn in turns],
        )
        unit_got += moved
        other.append(got)
        (grad_held if last else held).append(ahead)

    kept = {}

    def first_products(step):
        if step == 1:
            normed, hats = norm_blocks(rounds.begin(*held, *other), owners, gain, shift)
            normed, *unit_got[:] = rounds.begin(normed, *unit_got)
            kept["weight_out"] = gather(units.merge(output_weight, unit_got, bf16), "dp")
            qkv, activated, slope = hidden_units(normed, weight_in, bias_own, own)
            return dict(normed=normed, hats=hats, qkv=qkv, activated=activated, slope=slope)
        if step == 2:
            names = ("attended", "queries", "keys", "values", "stats")
            return dict(zip(names, attention_forward(rounds.begin(kept["qkv"]), own, stored, tables)))
        if step == 3:
            branch = jnp.concatenate(rounds.begin(kept["attended"], kept["activated"]), axis=1)
            return dict(branch=branch, out_part=dot(branch, kept["weight_out"], ((1,), (0,))).astype(bf16))
        return {}

    for step in range(1, far):
        source = rounds.begin(grad_held[step])
        started = [to_y(source)]
        if step < far - 1:
            started.append(to_z(source, 1))
        sends = len(started)
        made = first_products(step)
        started = rounds.end(*started, *made.values())
        kept.update(zip(made, started[sends:]))
        grad_other.append(started[0])
        grad_held += started[1:sends]
    normed, hats = kept["normed"], kept["hats"]
    branch, out_part, weight_out = kept["branch"], kept["out_part"], kept["weight_out"]
    out_sum = scatter(out_part, "ctx")
    grads = order_blocks(rounds.begin(*grad_held, *grad_other), owners)

    part = D // 4
    near = lambda r: lax.dynamic_slice_in_dim(normed, (dp_place ^ r) * part, part, 1)
    term = lambda r, chunk: dot(near(r), chunk, ((0,), (0,)))
    far_terms = lambda chunk: jnp.concatenate([term(1, chunk), term(3, chunk)]).astype(bf16)
    mid_terms = lambda chunk, got: (term(2, chunk) + got[part:].astype(f32)).astype(bf16)

    def near_terms(chunk, got, across):
        total = term(0, chunk) + got[:part].astype(f32) + across.astype(f32)
        return total.astype(bf16).reshape(count, part // count, -1)

    spread = lambda v: lax.all_to_all(v, "ctx", 0, 0, tiled=True)
    grad_up = (kept["slope"] * dot(grads, weight_out[own:], ((1,), (1,)))).astype(bf16)
    beside = to_core(far_terms(grad_up))
    grad_mix = dot(grads, weight_out[:own], ((1,), (1,))).astype(bf16)
    beside, grad_mix = rounds.end(beside, grad_mix)
    middle = mid_terms(grad_up, beside)
    middle, *saved = rounds.begin(middle, *[kept[name] for name in ("queries", "keys", "values", "stats")])
    across = to_x(middle)
    grad_qkv = attention_backward(
        saved,
        grad_mix,
        stored,
        tables,
    )
    grad_heads = jnp.concatenate(grad_qkv, axis=1)
    sent_heads = far_terms(grad_heads)
    across, sent_heads, *grad_qkv = rounds.end(across, sent_heads, *grad_qkv)

    sent_mlp, sent_heads, *grad_qkv = rounds.begin(near_terms(grad_up, beside, across), sent_heads, *grad_qkv)
    came_mlp = spread(sent_mlp)
    beside_heads = to_core(sent_heads)
    *normed_terms, sums = product_blocks([*grad_qkv, grad_up], weight_in, hats, owners, count)
    branch, sums = rounds.begin(branch, sums)
    out_term = dot(branch, grads, ((0,), (0,))).astype(bf16)
    out_near = lambda r: lax.dynamic_slice_in_dim(out_term, (dp_place ^ r) * rows_out, rows_out, 0)
    out_far = jnp.concatenate([out_near(1), out_near(3)])
    mid_heads = term(2, grad_heads)
    came_mlp, beside, out_term, out_far, mid_heads, sums, *normed_terms = rounds.end(
        came_mlp, beside_heads, out_term, out_far, mid_heads, sums, *normed_terms
    )

    bias_terms = [jnp.sum(v.astype(f32), axis=0) for v in grad_qkv]
    up_terms, at = jnp.sum(grad_up.astype(f32), axis=0), 0
    for _, width in column_pieces(0, count)[3:]:
        bias_terms.append(up_terms[at : at + width])
        at += width
    here = (jnp.arange(count) == place).astype(f32)[:, None]
    vector_terms = jnp.concatenate(
        [
            sums[0].reshape(devices, -1),
            sums[1].reshape(devices, -1),
            jnp.concatenate([(here * t[None]).reshape(-1) for t in bias_terms]).reshape(devices, -1),
            jnp.sum(grad_block.astype(f32), axis=0).reshape(devices, -1),
        ],
        axis=1,
    )
    small_left = small_steps()[::-1]

    def small_step(terms):
        axis, bit, upper = small_left.pop(0)
        give, keep = halve(terms, upper)
        return swap(give, axis, bit), keep

    mine, theirs = normed_terms[:far], normed_terms[far:]
    got, running = [None] * far, None
    back = Units(True, dp_place == 0)
    back_parts, back_got = [], []
    left_y, left_z, stage = list(range(far))[::-1], list(range(1, far))[::-1], 0
    across = came_heads = None
    while left_y or left_z or stage < 4:
        names, started = [], []

        def start(name, value):
            names.append(name)
            started.append(value)

        z_now = left_z[0] if left_z and got[left_z[0]] is not None else None
        pair = left_y[:2]
        left_y = left_y[2:]
        for k in pair:
            start(("y", k), to_y(rounds.begin(theirs[k])))
        if z_now is not None:
            left_z.pop(0)
            joint = mine[z_now] + got[z_now].astype(f32)
            if running is not None:
                joint = joint + running.astype(f32)
            start("z", to_z(rounds.begin(joint.astype(bf16)), -1))
        if stage == 0:
            middle = mid_heads + beside[part:].astype(f32)
            start("x", to_x(rounds.begin(middle.astype(bf16))))
            start("core", to_core(rounds.begin(out_far)))
        elif stage == 1:
            block_out = (token_block.astype(f32) + rounds.begin(out_sum).astype(f32) + bias_out).astype(bf16)
            start("block", block_out)
            start("spread", spread(rounds.begin(near_terms(grad_heads, beside, across))))
            middle = out_near(2).astype(f32) + out_beside[rows_out:].astype(f32)
            start("x", to_x(rounds.begin(middle.astype(bf16))))
        if stage == 2:
            out_own = out_near(0).astype(f32) + out_beside[:rows_out].astype(f32)
            out_own = (out_own + across.astype(f32)).astype(bf16)
            for part in back.split(out_own):
                start("part", part)
        elif stage == 3:
            back_parts = rounds.begin(*back_parts)
            for turn in range(5):
                start("unit", back.send(back_parts, turn))
        if small_left:
            give, keep = small_step(rounds.begin(vector_terms))
            start("give", give)
            start("keep", keep)
        stage += 1
        for name, value in zip(names, rounds.end(*started)):
            if name == "z":
                running = value
            elif name == "core":
                out_beside = value
            elif name == "block":
                block_out = value
            elif name == "x":
                across = value
            elif name == "spread":
                came_heads = value
            elif name == "part":
                back_parts.append(value)
            elif name == "unit":
                back_got.append(value)
            elif name == "give":
                vector_terms = value
            elif name == "keep":
                vector_terms = vector_terms + value
            else:
                got[name[1]] = value
    joined = lambda step: mine[step] + got[step].astype(f32)
    weightin_grad = join_columns([came_heads, came_mlp], [slice(0, 3), slice(3, None)], count)
    weightout_grad = back.merge(out_own, back_got, f32)
    while small_left:
        give, keep = small_step(vector_terms)
        vector_terms = give + keep
    gain_grad, shift_grad, biasin_grad, biasout_grad = (
        vector_terms[0, end - cut : end] for cut, end in zip(cuts, ends)
    )

    own_normed = joined(0) + running.astype(f32)
    own_x = token_block.astype(f32)
    centred = own_x - jnp.mean(own_x, axis=-1, keepdims=True)
    scale = lax.rsqrt(jnp.mean(centred * centred, axis=-1, keepdims=True) + epsilon)
    hat = centred * scale
    g = own_normed * gain
    tokens_grad = rounds.thread.astype(f32) + scale * (
        g - jnp.mean(g, axis=-1, keepdims=True) - hat * jnp.mean(g * hat, axis=-1, keepdims=True)
    )
    return (
        block_out.reshape(tokens.shape),
        tokens_grad.reshape(tokens.shape),
        gain_grad,
        shift_grad,
        weightin_grad,
        biasin_grad,
        weightout_grad,
        biasout_grad,
    )


def solution(mesh):
    placed = (
        P("dp", None, "ctx", None, None),
        P(("dp", "ctx")),
        P(("dp", "ctx")),
        P(("dp", "ctx"), None),
        P(("dp", "ctx")),
        P(("dp", "ctx"), None),
        P(("dp", "ctx")),
        P("dp", None, "ctx", None, None),
    )
    return jax.shard_map(
        local,
        mesh=mesh,
        in_specs=placed,
        out_specs=(
            P("dp", None, "ctx", None, None),
            P("dp", None, "ctx", None, None),
            P(("dp", "ctx")),
            P(("dp", "ctx")),
            P(("dp", "ctx"), None),
            P(("dp", "ctx")),
            P(("dp", "ctx"), None),
            P(("dp", "ctx")),
        ),
        check_vma=False,
    )
```

```python
import functools
import math

import jax
import jax.numpy as jnp
from jax import lax
from jax.experimental import pallas as pl
from jax.experimental.pallas import tpu as pltpu
from jax.sharding import PartitionSpec as P

D = 2048
HEADS = 32
HEAD = 64
ROT = 32
BLK = 64
FF = 8192
TILE = 256

epsilon = 1e-05
theta_log = math.log(10000.0)
masked_fill = -1e30
bf16 = jnp.bfloat16
f32 = jnp.float32


def dot(a, b, dims):
    return lax.dot_general(a, b, (dims, ((), ())), preferred_element_type=f32)


def whole(shape, dtype):
    return jax.ShapeDtypeStruct(shape, dtype)


VMEM = pl.BlockSpec(memory_space=pltpu.VMEM)
SMEM = pl.BlockSpec(memory_space=pltpu.SMEM)
ROOM = pltpu.CompilerParams(vmem_limit_bytes=56 * 2**20)
LIGHT = pl.CostEstimate(flops=1, bytes_accessed=1, transcendentals=0)


def turn_lanes(values, cos, sin, sign):
    half = ROT // 2
    width = values.shape[-1]
    place = lax.broadcasted_iota(jnp.int32, (1, width), 1) % HEAD
    ahead = pltpu.roll(values, width - half, 1)
    behind = pltpu.roll(values, half, 1)
    turned = values * cos + sign * sin * jnp.where(place < half, -ahead, behind)
    return jnp.where(place < ROT, turned, values)


def head_scores(keys, q_head, start, reach, tile):
    scores = dot(keys, q_head * 0.125, ((1,), (1,)))
    if isinstance(start, int):
        before, start, reach = scores[:start], 0, reach - start
        scores = scores[-reach:]
    else:
        before = scores[:0]
    allowed = lax.broadcasted_iota(jnp.int32, (reach, tile), 0) <= start + (
        lax.broadcasted_iota(jnp.int32, (reach, tile), 1)
    )
    scores = jnp.where(allowed, scores, masked_fill)
    return jnp.concatenate([before, scores]) if before.shape[0] else scores


def for_row_tiles(length, tile, body):
    count = length // tile
    if count <= 4:
        for step in range(count):
            body(step * tile, (step + 1) * tile)
    else:
        per = count // 4
        for part in range(4):

            @pl.loop(part * per, (part + 1) * per)
            def _(step, part=part):
                body(pl.multiple_of(step * tile, tile), (part + 1) * per * tile)


def forward_kernel(length, width, stored, hq, hk, hv, cos, sin, att, qs, ks, vs, stats, raw, vt):
    lanes = lax.broadcasted_iota(jnp.int32, (1, width), 1)
    tile = min(TILE, length)
    blocks = length // BLK
    cos_all, sin_all = cos[...], sin[...]

    def natural(ref):
        for b in range(blocks):
            raw[b * BLK : (b + 1) * BLK, :] = ref[stored[b] : stored[b] + BLK, :]
        return raw[...]

    qs[...] = turn_lanes(natural(hq), cos_all, sin_all, 1.0).astype(bf16)
    ks[...] = turn_lanes(natural(hk), cos_all, sin_all, 1.0).astype(bf16)
    values = natural(hv)
    vs[...] = values.astype(bf16)
    vt[...] = values.T.astype(bf16)

    def body(start, reach):
        rows = pl.ds(start, tile)
        q_rows = qs[rows, :]
        keys = ks[0:reach, :]
        mixes = []
        for head in range(width // HEAD):
            mine = (lanes // HEAD) == head
            q_head = jnp.where(mine, q_rows, jnp.zeros_like(q_rows))
            scores = head_scores(keys, q_head, start, reach, tile)
            top = jnp.max(scores, axis=0, keepdims=True)
            weights = jnp.exp(scores - top)
            part = 1.0 / jnp.sum(weights, axis=0, keepdims=True)
            stats[0, 2 * head : 2 * head + 1, rows] = top
            stats[0, 2 * head + 1 : 2 * head + 2, rows] = part
            low = (weights * part).astype(bf16)
            mixes.append(dot(vt[head * HEAD : (head + 1) * HEAD, 0:reach], low, ((1,), (0,))))
        raw[rows, :] = jnp.concatenate(mixes, axis=0).T

    for_row_tiles(length, tile, body)
    for b in range(blocks):
        att[stored[b] : stored[b] + BLK, :] = raw[b * BLK : (b + 1) * BLK, :].astype(bf16)


def backward_kernel(length, width, stored, qs, ks, vs, stats, gm, cos, sin, gq, gk, gv, gs, kt, dq, dk, dv):
    lanes = lax.broadcasted_iota(jnp.int32, (1, width), 1)
    tile = min(TILE, length)
    blocks = length // BLK
    for b in range(blocks):
        gs[b * BLK : (b + 1) * BLK, :] = gm[stored[b] : stored[b] + BLK, :]
    kt[...] = ks[...].T
    dk[...] = jnp.zeros_like(dk)
    dv[...] = jnp.zeros_like(dv)

    def body(start, reach):
        rows = pl.ds(start, tile)
        q_rows = qs[rows, :]
        g_rows = gs[rows, :]
        keys = ks[0:reach, :]
        vals = vs[0:reach, :]
        gqs = []
        for head in range(width // HEAD):
            mine = (lanes // HEAD) == head
            q_head = jnp.where(mine, q_rows, jnp.zeros_like(q_rows))
            g_head = jnp.where(mine, g_rows, jnp.zeros_like(g_rows))
            scores = head_scores(keys, q_head, start, reach, tile)
            top = stats[0, 2 * head : 2 * head + 1, rows]
            part = stats[0, 2 * head + 1 : 2 * head + 2, rows]
            shares = jnp.exp(scores - top) * part
            grad_shares = dot(vals, g_head, ((1,), (1,)))
            moved = shares * grad_shares
            inner = jnp.sum(moved, axis=0, keepdims=True)
            grad_scores = (moved - shares * inner).astype(bf16)
            gqs.append(dot(kt[head * HEAD : (head + 1) * HEAD, 0:reach], grad_scores, ((1,), (0,))))
            dv[0:reach, :] += dot(shares.astype(bf16), g_head, ((1,), (0,)))
            dk[0:reach, :] += dot(grad_scores, q_head, ((1,), (0,)))
        grad_q = jnp.concatenate(gqs, axis=0).T * 0.125
        dq[rows, :] = turn_lanes(grad_q, cos[rows, :], sin[rows, :], -1.0).astype(bf16)

    for_row_tiles(length, tile, body)
    grad_k = turn_lanes(dk[...] * 0.125, cos[...], sin[...], -1.0).astype(bf16)
    grad_v = dv[...].astype(bf16)
    for b in range(blocks):
        here, there = slice(b * BLK, (b + 1) * BLK), slice(stored[b], stored[b] + BLK)
        gq[there, :] = dq[here, :]
        gk[there, :] = grad_k[here]
        gv[there, :] = grad_v[here]


def rotary_tables(length, width):
    frequency = jnp.exp(-theta_log * 2.0 * jnp.arange(ROT // 2).astype(f32) / ROT)
    angles = jnp.arange(length, dtype=jnp.int32).astype(f32)[:, None] * frequency[None, :]
    spare = jnp.zeros((length, HEAD - ROT), f32)
    repeat = width // HEAD
    cos = jnp.tile(jnp.concatenate([jnp.cos(angles)] * 2 + [spare], axis=1), (1, repeat))
    sin = jnp.tile(jnp.concatenate([jnp.sin(angles)] * 2 + [spare], axis=1), (1, repeat))
    return cos, sin


def attention_specs(length, columns):
    width = min(128, columns)
    groups = columns // width
    group = pl.BlockSpec((length, width), lambda g: (0, g))
    table = pl.BlockSpec((length, width), lambda g: (0, 0))
    stats = pl.BlockSpec((1, 8, length), lambda g: (g, 0, 0))
    return width, groups, group, table, stats


def attention_forward(hidden, columns, stored, tables):
    length = hidden.shape[0]
    width, groups, group, table, stats = attention_specs(length, columns)
    if width < 128:
        parts = [hidden[:, k * columns : (k + 1) * columns] for k in range(3)]
        specs = [group] * 3
    else:
        parts = [hidden] * 3
        specs = [pl.BlockSpec((length, width), lambda g, k=k: (0, k * groups + g)) for k in range(3)]
    return pl.pallas_call(
        functools.partial(forward_kernel, length, width, stored),
        grid=(groups,),
        in_specs=specs + [table, table],
        out_specs=[group] * 4 + [stats],
        out_shape=[whole((length, columns), bf16)] * 4 + [whole((groups, 8, length), f32)],
        scratch_shapes=[pltpu.VMEM((length, width), f32), pltpu.VMEM((width, length), bf16)],
        compiler_params=ROOM,
        cost_estimate=LIGHT,
        name="attention_forward",
    )(*parts, *tables)


def attention_backward(kept, grad_mix, stored, tables):
    length, columns = grad_mix.shape
    width, groups, group, table, stats = attention_specs(length, columns)
    return pl.pallas_call(
        functools.partial(backward_kernel, length, width, stored),
        grid=(groups,),
        in_specs=[group] * 3 + [stats, group, table, table],
        out_specs=[group] * 3,
        out_shape=[whole((length, columns), bf16)] * 3,
        scratch_shapes=[
            pltpu.VMEM((length, width), bf16),
            pltpu.VMEM((width, length), bf16),
            pltpu.VMEM((length, width), bf16),
            pltpu.VMEM((length, width), f32),
            pltpu.VMEM((length, width), f32),
        ],
        compiler_params=ROOM,
        cost_estimate=LIGHT,
        name="attention_backward",
    )(*kept, grad_mix, *tables)


def norm_kernel(owners, gain, shift, *refs):
    blocks, (normed, hats) = refs[:-2], refs[-2:]
    rows = blocks[0].shape[0]
    for b, ref in enumerate(blocks):
        x = ref[...].astype(f32)
        centred = x - jnp.mean(x, axis=-1, keepdims=True)
        hat = centred * lax.rsqrt(jnp.mean(centred * centred, axis=-1, keepdims=True) + epsilon)
        there = pl.ds(pl.multiple_of(owners[b] * rows, rows), rows)
        normed[there, :] = (hat * gain[...] + shift[...]).astype(bf16)
        hats[there, :] = hat.astype(bf16)


def norm_blocks(blocks, owners, gain, shift):
    rows = blocks[0].shape[0]
    total = rows * len(blocks)
    if total > 1024:
        normed = hats = jnp.zeros((total, D), bf16)
        for b, block in enumerate(blocks):
            x = block.astype(f32)
            centred = x - jnp.mean(x, axis=-1, keepdims=True)
            spread = jnp.mean(centred * centred, axis=-1, keepdims=True)
            hat = centred * lax.rsqrt(spread + epsilon)
            at = (owners[b] * rows, 0)
            normed = lax.dynamic_update_slice(normed, (hat * gain + shift).astype(bf16), at)
            hats = lax.dynamic_update_slice(hats, hat.astype(bf16), at)
        return normed, hats
    return pl.pallas_call(
        norm_kernel,
        in_specs=[SMEM] + [VMEM] * (2 + len(blocks)),
        out_specs=[VMEM] * 2,
        out_shape=[whole((total, D), bf16)] * 2,
        compiler_params=ROOM,
        cost_estimate=LIGHT,
        name="norm",
    )(owners, gain[None], shift[None], *blocks)


def order_kernel(owners, *refs):
    *blocks, out = refs
    rows = blocks[0].shape[0]
    for b, ref in enumerate(blocks):
        out[pl.ds(pl.multiple_of(owners[b] * rows, rows), rows), :] = ref[...]


def order_blocks(blocks, owners):
    rows, columns = blocks[0].shape
    return pl.pallas_call(
        order_kernel,
        in_specs=[SMEM] + [VMEM] * len(blocks),
        out_specs=VMEM,
        out_shape=whole((rows * len(blocks), columns), blocks[0].dtype),
        compiler_params=ROOM,
        cost_estimate=LIGHT,
        name="order_blocks",
    )(owners, *blocks)


def hidden_kernel(heads, normed, weight, bias, qkv, activated, slope):
    step = pl.program_id(0)
    rows = normed.shape[0]
    blocks = [slice(at, at + rows) for at in range(0, normed.shape[0], rows)]

    @pl.when(step < heads)
    def _():
        for span in blocks:
            qkv[span, :] = dot(normed[span, :], weight[...], ((1,), (0,))) + bias[...]

    @pl.when(step >= heads)
    def _():
        for span in blocks:
            v = dot(normed[span, :], weight[...], ((1,), (0,))) + bias[...]
            squared = v * v
            bend = jnp.tanh(0.7978845608 * v * (1.0 + 0.044715 * squared))
            half = 0.5 * (1.0 + bend)
            activated[span, :] = (v * half).astype(bf16)
            inner = 0.7978845608 * (1.0 + 3 * 0.044715 * squared)
            slope[span, :] = half + 0.5 * v * (1.0 - bend * bend) * inner


def hidden_units(normed, weight, bias, own):
    length, tile = normed.shape[0], 256
    heads = 3 * own // tile
    rest = weight.shape[1] - 3 * own
    if 3 * own % tile or rest % tile or length > 1024:
        gelu = lambda v: jax.nn.gelu(v, approximate=True)
        hidden = dot(normed, weight, ((1,), (0,))) + bias
        activated, slope = jax.jvp(
            gelu, (hidden[:, 3 * own :],), (jnp.ones((length, rest), f32),)
        )
        return hidden[:, : 3 * own], activated.astype(bf16), slope
    late = pl.BlockSpec((length, tile), lambda n: (0, jnp.maximum(n - heads, 0)))
    return pl.pallas_call(
        functools.partial(hidden_kernel, heads),
        grid=(weight.shape[1] // tile,),
        in_specs=[
            pl.BlockSpec((length, D), lambda n: (0, 0)),
            pl.BlockSpec((D, tile), lambda n: (0, n)),
            pl.BlockSpec((1, tile), lambda n: (0, n)),
        ],
        out_specs=[
            pl.BlockSpec((length, tile), lambda n: (0, jnp.minimum(n, heads - 1))),
            late,
            late,
        ],
        out_shape=[whole((length, 3 * own), f32), whole((length, rest), bf16), whole((length, rest), f32)],
        compiler_params=ROOM,
        cost_estimate=LIGHT,
        name="hidden_units",
    )(normed, weight, bias[None])


def column_pieces(index, count):
    own = D // count
    rows = (D + FF) // (4 * count)
    pieces = [(which * D + index * own, own) for which in range(3)]
    pieces.append((3 * D + index * (rows - own), rows - own))
    for part in range(1, 4):
        pieces.append((3 * D + part * rows * count - D + index * rows, rows))
    return pieces


def split_kernel(count, weight, out):
    for index in range(count):
        at = 0
        for start, width in column_pieces(index, count):
            out[index, :, at : at + width] = weight[:, start : start + width]
            at += width


def split_columns(weight, count):
    rows, columns = weight.shape
    return pl.pallas_call(
        functools.partial(split_kernel, count),
        in_specs=[VMEM],
        out_specs=VMEM,
        out_shape=whole((count, rows, columns // count), weight.dtype),
        compiler_params=ROOM,
        cost_estimate=LIGHT,
        name="split_columns",
    )(weight)


def join_kernel(count, spans, *refs):
    *splits, out = refs
    for split, span in zip(splits, spans):
        for index in range(count):
            at = 0
            for start, width in column_pieces(index, count)[span]:
                out[:, start : start + width] = split[index, :, at : at + width].astype(f32)
                at += width


def join_columns(splits, spans, count):
    rows = splits[0].shape[1]
    return pl.pallas_call(
        functools.partial(join_kernel, count, spans),
        in_specs=[VMEM] * len(splits),
        out_specs=VMEM,
        out_shape=whole((rows, 3 * D + FF), f32),
        compiler_params=ROOM,
        cost_estimate=LIGHT,
        name="join_columns",
    )(*splits)


def product_kernel(number, owners, *refs):
    parts, (weight, hats), (*outs, sums) = refs[:number], refs[number : number + 2], refs[number + 2 :]
    rows = outs[0].shape[0]
    half = len(outs) // 2
    gain = shift = 0.0
    for low in (half, 0):
        there = [
            pl.ds(pl.multiple_of(owners[low + k] * rows, rows), rows) for k in range(half)
        ]
        total, at = None, 0
        for part in parts:
            size = part.shape[1]
            taken = jnp.concatenate([part[rows_k, :] for rows_k in there])
            term = dot(taken, weight[:, at : at + size], ((1,), (1,)))
            total = term if total is None else total + term
            at += size
        hat = jnp.concatenate([hats[rows_k, :] for rows_k in there]).astype(f32)
        gain += jnp.sum(total * hat, axis=0, keepdims=True)
        shift += jnp.sum(total, axis=0, keepdims=True)
        for k in range(half):
            out = outs[low + k]
            out[...] = total[k * rows : (k + 1) * rows].astype(out.dtype)
    sums[0:1, :] = gain
    sums[1:2, :] = shift


def product_blocks(parts, weight, hats, owners, count):
    rows = parts[0].shape[0] // count
    depth = sum(part.shape[1] for part in parts)
    tile = D // 4
    return pl.pallas_call(
        functools.partial(product_kernel, len(parts)),
        grid_spec=pltpu.PrefetchScalarGridSpec(
            num_scalar_prefetch=1,
            grid=(D // tile,),
            in_specs=[pl.BlockSpec(part.shape, lambda n, *_: (0, 0)) for part in parts]
            + [
                pl.BlockSpec((tile, depth), lambda n, *_: (n, 0)),
                pl.BlockSpec((rows * count, tile), lambda n, *_: (0, n)),
            ],
            out_specs=[pl.BlockSpec((rows, tile), lambda n, *_: (0, n))] * count
            + [pl.BlockSpec((8, tile), lambda n, *_: (0, n))],
        ),
        out_shape=[whole((rows, D), f32)] * (count // 2)
        + [whole((rows, D), bf16)] * (count // 2)
        + [whole((8, D), f32)],
        compiler_params=ROOM,
        cost_estimate=LIGHT,
        name="product_blocks",
    )(owners, *parts, weight, hats)


class Rounds:
    def __init__(self, thread):
        self.thread = thread

    def pass_through(self, *values):
        *values, self.thread = lax.optimization_barrier((*values, self.thread))
        return tuple(values)

    def begin(self, *values):
        values = self.pass_through(*values)
        return values[0] if len(values) == 1 else values

    def end(self, *values):
        return self.pass_through(*values)


def shift_pairs(size, by):
    return [(k, (k + by) % size) for k in range(size)]


def flip_pairs(size, bit):
    return [(k, k ^ bit) for k in range(size)]


def to_y(value):
    return lax.ppermute(value, "ctx", flip_pairs(lax.axis_size("ctx"), 1))


def to_z(value, by):
    return lax.ppermute(value, "ctx", shift_pairs(lax.axis_size("ctx"), 2 * by))


def to_x(value):
    return lax.ppermute(value, "dp", flip_pairs(4, 2))


def to_core(value):
    return lax.ppermute(value, "dp", flip_pairs(4, 1))


def small_steps():
    steps = []
    for axis in ("ctx", "dp"):
        bit = 1
        while bit < lax.axis_size(axis):
            steps.append((axis, bit, (lax.axis_index(axis) & bit) != 0))
            bit *= 2
    return steps


def swap(value, axis, bit):
    return lax.ppermute(value, axis, flip_pairs(lax.axis_size(axis), bit))


def halve(held, upper):
    half = held.shape[0] // 2
    low, high = held[:half], held[half:]
    return jnp.where(upper, low, high), jnp.where(upper, high, low)


def unit_rounds(count):
    edges = []
    for m in range(5 * count):
        owner, slot = (m // 4, m % 4) if m < 4 * count else (m - 4 * count, 4)
        edges.append((m // 5, m % 5, owner, slot))
    rounds = []
    left = list(edges)
    for _ in range(5):
        by_source = [[e for e in left if e[0] == s] for s in range(count)]
        taken = {}

        def place_edge(source, seen):
            for edge in by_source[source]:
                if edge[2] in seen:
                    continue
                seen.add(edge[2])
                if edge[2] not in taken or place_edge(taken[edge[2]][0], seen):
                    taken[edge[2]] = edge
                    return True
            return False

        for source in range(count):
            assert place_edge(source, set())
        chosen = {edge[0]: edge for edge in taken.values()}
        rounds.append([chosen[s] for s in range(count)])
        for edge in taken.values():
            left.remove(edge)
    return rounds


def unit_table(count, back):
    table, rounds = [[0] * 10 for _ in range(count)], []
    for turn, chosen in enumerate(unit_rounds(count)):
        pairs = []
        for source, unit, owner, slot in chosen:
            if back:
                source, unit, owner, slot = owner, slot, source, unit
            pairs.append((source, owner))
            table[source][turn] = unit
            table[owner][5 + turn] = slot
        rounds.append(pairs)
    return jnp.array(table, jnp.int32), rounds


def unit_out_kernel(units, block, *outs):
    rows = outs[0].shape[0]
    for turn, out in enumerate(outs):
        out[...] = block[pl.ds(pl.multiple_of(units[turn] * rows, rows), rows), :]


def unit_in_kernel(units, first, block, *refs):
    *gots, out = refs
    rows = gots[0].shape[0]

    @pl.when(first[0] == 1)
    def _():
        for turn, got in enumerate(gots):
            at = pl.multiple_of(units[5 + turn] * rows, rows)
            out[pl.ds(at, rows), :] = got[...].astype(out.dtype)

    @pl.when(first[0] == 0)
    def _():
        out[...] = block[...].astype(out.dtype)


class Units:
    def __init__(self, back, first):
        self.count = lax.axis_size("ctx")
        table, self.rounds = unit_table(self.count, back)
        self.units = table[lax.axis_index("ctx")]
        self.first = first.astype(jnp.int32)[None]

    def split(self, block):
        rows, columns = block.shape
        return pl.pallas_call(
            unit_out_kernel,
            in_specs=[SMEM, VMEM],
            out_specs=[VMEM] * 5,
            out_shape=[whole((rows // 5, columns), bf16)] * 5,
            compiler_params=ROOM,
            cost_estimate=LIGHT,
            name="unit_out",
        )(self.units, block)

    def send(self, parts, turn):
        return lax.ppermute(parts[turn], ("dp", "ctx"), self.rounds[turn])

    def merge(self, block, got, dtype):
        return pl.pallas_call(
            unit_in_kernel,
            in_specs=[SMEM, SMEM] + [VMEM] * 6,
            out_specs=VMEM,
            out_shape=whole(block.shape, dtype),
            compiler_params=ROOM,
            cost_estimate=LIGHT,
            name="unit_in",
        )(self.units, self.first, block, *got)


def local(
    tokens, norm_gain, norm_shift, input_weight, input_bias, output_weight, output_bias, cotangent
):
    count = lax.axis_size("ctx")
    place = lax.axis_index("ctx")
    dp_place = lax.axis_index("dp")
    far = count // 2
    z, y = place // 2, place % 2
    devices = 4 * count
    own = D // count
    length = 2 * BLK * count
    rows_out = output_weight.shape[0]
    token_block = tokens.reshape(2 * BLK, D)
    grad_block = cotangent.reshape(2 * BLK, D)

    stored = [min(b, 2 * count - 1 - b) * 2 * BLK + BLK * (b >= count) for b in range(2 * count)]
    steps = jnp.arange(far, dtype=jnp.int32)
    owners_mine = ((z + far - steps) % far) * 2 + y
    owners = jnp.concatenate([owners_mine, owners_mine ^ 1])
    rounds = Rounds(grad_block)
    gather = lambda v, axis: lax.all_gather(v, axis, axis=0, tiled=True)
    scatter = lambda v, axis: lax.psum_scatter(v, axis, scatter_dimension=0, tiled=True)

    small = jnp.concatenate([norm_gain, norm_shift, input_bias, output_bias])
    cuts = [norm_gain.shape[0], norm_shift.shape[0], input_bias.shape[0], output_bias.shape[0]]
    ends = [sum(cuts[: k + 1]) for k in range(4)]
    units = Units(False, dp_place == 0)
    packed = split_columns(input_weight, count)
    held, other = [token_block, to_z(token_block, 1)], [to_y(token_block)]
    grad_held, grad_other = [grad_block], [to_y(grad_block)]
    columns = lax.all_to_all(packed, "ctx", 0, 0, tiled=True)
    unit_parts = units.split(output_weight)
    unit_got = []
    tables = rotary_tables(length, min(128, own))
    vectors = small[None]
    for axis, bit, upper in small_steps():
        got = swap(vectors, axis, bit)
        vectors = jnp.where(
            upper, jnp.concatenate([got, vectors]), jnp.concatenate([vectors, got])
        )
    tables = tuple(tables)
    first = rounds.end(held[1], other[0], grad_other[0], columns, vectors, *tables, *unit_parts)
    held[1], other[0], grad_other[0], columns, vectors, *tables = first[:7]
    unit_parts = first[7:]
    weight_in = gather(columns.reshape(-1, columns.shape[-1]), "dp")
    gain, shift, bias_in, bias_out = (
        vectors[:, end - cut : end].reshape(-1).astype(f32) for cut, end in zip(cuts, ends)
    )
    bias_own = jnp.concatenate(
        [lax.dynamic_slice_in_dim(bias_in, start, width) for start, width in column_pieces(place, count)]
    )

    for step in range(1, far):
        last = step == far - 1
        source = rounds.begin(held[step])
        turns = range(len(unit_got), 5 if last else min(5, len(unit_got) + 2))
        got, ahead, *moved = rounds.end(
            to_y(source),
            to_z(rounds.begin(grad_block) if last else source, 1),
            *[units.send(rounds.begin(*unit_parts), turn) for turn in turns],
        )
        unit_got += moved
        other.append(got)
        (grad_held if last else held).append(ahead)

    kept = {}

    def first_products(step):
        if step == 1:
            normed, hats = norm_blocks(rounds.begin(*held, *other), owners, gain, shift)
            normed, *unit_got[:] = rounds.begin(normed, *unit_got)
            kept["weight_out"] = gather(units.merge(output_weight, unit_got, bf16), "dp")
            qkv, activated, slope = hidden_units(normed, weight_in, bias_own, own)
            return dict(normed=normed, hats=hats, qkv=qkv, activated=activated, slope=slope)
        if step == 2:
            names = ("attended", "queries", "keys", "values", "stats")
            return dict(zip(names, attention_forward(rounds.begin(kept["qkv"]), own, stored, tables)))
        if step == 3:
            branch = jnp.concatenate(rounds.begin(kept["attended"], kept["activated"]), axis=1)
            return dict(branch=branch, out_part=dot(branch, kept["weight_out"], ((1,), (0,))).astype(bf16))
        return {}

    for step in range(1, far):
        source = rounds.begin(grad_held[step])
        started = [to_y(source)]
        if step < far - 1:
            started.append(to_z(source, 1))
        sends = len(started)
        made = first_products(step)
        started = rounds.end(*started, *made.values())
        kept.update(zip(made, started[sends:]))
        grad_other.append(started[0])
        grad_held += started[1:sends]
    normed, hats = kept["normed"], kept["hats"]
    branch, out_part, weight_out = kept["branch"], kept["out_part"], kept["weight_out"]
    out_sum = scatter(out_part, "ctx")
    grads = order_blocks(rounds.begin(*grad_held, *grad_other), owners)

    part = D // 4
    near = lambda r: lax.dynamic_slice_in_dim(normed, (dp_place ^ r) * part, part, 1)
    term = lambda r, chunk: dot(near(r), chunk, ((0,), (0,)))
    normed_far = jnp.concatenate([near(1), near(3)], axis=1)
    far_terms = lambda chunk: dot(normed_far, chunk, ((0,), (0,))).astype(bf16)
    mid_terms = lambda chunk, got: (term(2, chunk) + got[part:].astype(f32)).astype(bf16)

    def near_terms(chunk, got, across):
        total = term(0, chunk) + got[:part].astype(f32) + across.astype(f32)
        return total.astype(bf16).reshape(count, part // count, -1)

    spread = lambda v: lax.all_to_all(v, "ctx", 0, 0, tiled=True)
    grad_up = (kept["slope"] * dot(grads, weight_out[own:], ((1,), (1,)))).astype(bf16)
    beside = to_core(far_terms(grad_up))
    grad_mix = dot(grads, weight_out[:own], ((1,), (1,))).astype(bf16)
    beside, grad_mix = rounds.end(beside, grad_mix)
    middle = mid_terms(grad_up, beside)
    middle, *saved = rounds.begin(middle, *[kept[name] for name in ("queries", "keys", "values", "stats")])
    across = to_x(middle)
    grad_qkv = attention_backward(
        saved,
        grad_mix,
        stored,
        tables,
    )
    grad_heads = jnp.concatenate(grad_qkv, axis=1)
    sent_heads = far_terms(grad_heads)
    across, sent_heads, *grad_qkv = rounds.end(across, sent_heads, *grad_qkv)

    sent_mlp, sent_heads, *grad_qkv = rounds.begin(near_terms(grad_up, beside, across), sent_heads, *grad_qkv)
    came_mlp = spread(sent_mlp)
    beside_heads = to_core(sent_heads)
    *normed_terms, sums = product_blocks([*grad_qkv, grad_up], weight_in, hats, owners, count)
    branch, sums = rounds.begin(branch, sums)
    out_term = dot(branch, grads, ((0,), (0,))).astype(bf16)
    out_near = lambda r: lax.dynamic_slice_in_dim(out_term, (dp_place ^ r) * rows_out, rows_out, 0)
    out_far = jnp.concatenate([out_near(1), out_near(3)])
    mid_heads = term(2, grad_heads)
    came_mlp, beside, out_term, out_far, mid_heads, sums, *normed_terms = rounds.end(
        came_mlp, beside_heads, out_term, out_far, mid_heads, sums, *normed_terms
    )

    bias_terms = [jnp.sum(v.astype(f32), axis=0) for v in grad_qkv]
    up_terms, at = jnp.sum(grad_up.astype(f32), axis=0), 0
    for _, width in column_pieces(0, count)[3:]:
        bias_terms.append(up_terms[at : at + width])
        at += width
    here = (jnp.arange(count) == place).astype(f32)[:, None]
    vector_terms = jnp.concatenate(
        [
            sums[0].reshape(devices, -1),
            sums[1].reshape(devices, -1),
            jnp.concatenate([(here * t[None]).reshape(-1) for t in bias_terms]).reshape(devices, -1),
            jnp.sum(grad_block.astype(f32), axis=0).reshape(devices, -1),
        ],
        axis=1,
    )
    small_left = small_steps()[::-1]

    def small_step(terms):
        axis, bit, upper = small_left.pop(0)
        give, keep = halve(terms, upper)
        return swap(give, axis, bit), keep

    mine, theirs = normed_terms[:far], normed_terms[far:]
    got, running = [None] * far, None
    back = Units(True, dp_place == 0)
    back_parts, back_got = [], []
    left_y, left_z, stage = list(range(far))[::-1], list(range(1, far))[::-1], 0
    across = came_heads = None
    while left_y or left_z or stage < 4:
        names, started = [], []

        def start(name, value):
            names.append(name)
            started.append(value)

        z_now = left_z[0] if left_z and got[left_z[0]] is not None else None
        pair = left_y[:2]
        left_y = left_y[2:]
        for k in pair:
            start(("y", k), to_y(rounds.begin(theirs[k])))
        if z_now is not None:
            left_z.pop(0)
            joint = mine[z_now] + got[z_now].astype(f32)
            if running is not None:
                joint = joint + running.astype(f32)
            start("z", to_z(rounds.begin(joint.astype(bf16)), -1))
        if stage == 0:
            middle = mid_heads + beside[part:].astype(f32)
            start("x", to_x(rounds.begin(middle.astype(bf16))))
            start("core", to_core(rounds.begin(out_far)))
        elif stage == 1:
            block_out = (token_block.astype(f32) + rounds.begin(out_sum).astype(f32) + bias_out).astype(bf16)
            start("block", block_out)
            start("spread", spread(rounds.begin(near_terms(grad_heads, beside, across))))
            middle = out_near(2).astype(f32) + out_beside[rows_out:].astype(f32)
            start("x", to_x(rounds.begin(middle.astype(bf16))))
        if stage == 2:
            out_own = out_near(0).astype(f32) + out_beside[:rows_out].astype(f32)
            out_own = (out_own + across.astype(f32)).astype(bf16)
            for part in back.split(out_own):
                start("part", part)
        elif stage == 3:
            back_parts = rounds.begin(*back_parts)
            for turn in range(5):
                start("unit", back.send(back_parts, turn))
        if small_left:
            give, keep = small_step(rounds.begin(vector_terms))
            start("give", give)
            start("keep", keep)
        stage += 1
        for name, value in zip(names, rounds.end(*started)):
            if name == "z":
                running = value
            elif name == "core":
                out_beside = value
            elif name == "block":
                block_out = value
            elif name == "x":
                across = value
            elif name == "spread":
                came_heads = value
            elif name == "part":
                back_parts.append(value)
            elif name == "unit":
                back_got.append(value)
            elif name == "give":
                vector_terms = value
            elif name == "keep":
                vector_terms = vector_terms + value
            else:
                got[name[1]] = value
    joined = lambda step: mine[step] + got[step].astype(f32)
    weightin_grad = join_columns([came_heads, came_mlp], [slice(0, 3), slice(3, None)], count)
    weightout_grad = back.merge(out_own, back_got, f32)
    while small_left:
        give, keep = small_step(vector_terms)
        vector_terms = give + keep
    gain_grad, shift_grad, biasin_grad, biasout_grad = (
        vector_terms[0, end - cut : end] for cut, end in zip(cuts, ends)
    )

    own_normed = joined(0) + running.astype(f32)
    own_x = token_block.astype(f32)
    centred = own_x - jnp.mean(own_x, axis=-1, keepdims=True)
    scale = lax.rsqrt(jnp.mean(centred * centred, axis=-1, keepdims=True) + epsilon)
    hat = centred * scale
    g = own_normed * gain
    tokens_grad = rounds.thread.astype(f32) + scale * (
        g - jnp.mean(g, axis=-1, keepdims=True) - hat * jnp.mean(g * hat, axis=-1, keepdims=True)
    )
    return (
        block_out.reshape(tokens.shape),
        tokens_grad.reshape(tokens.shape),
        gain_grad,
        shift_grad,
        weightin_grad,
        biasin_grad,
        weightout_grad,
        biasout_grad,
    )


def solution(mesh):
    placed = (
        P("dp", None, "ctx", None, None),
        P(("dp", "ctx")),
        P(("dp", "ctx")),
        P(("dp", "ctx"), None),
        P(("dp", "ctx")),
        P(("dp", "ctx"), None),
        P(("dp", "ctx")),
        P("dp", None, "ctx", None, None),
    )
    return jax.shard_map(
        local,
        mesh=mesh,
        in_specs=placed,
        out_specs=(
            P("dp", None, "ctx", None, None),
            P("dp", None, "ctx", None, None),
            P(("dp", "ctx")),
            P(("dp", "ctx")),
            P(("dp", "ctx"), None),
            P(("dp", "ctx")),
            P(("dp", "ctx"), None),
            P(("dp", "ctx")),
        ),
        check_vma=False,
    )
```
